32 devices in a mesh: elem: 8 (over z, x), band: 4 (over y, core).
Axes of the slice: x: 2, y: 2, z: 4, core: 2. Of those that a mesh axis runs over, the one named last changes fastest.
Arguments:
- crm_state: bfloat16 [8, 128, 6, 3840], P('elem', 'band'), may hold values from -6 to 6
- host_state: float32 [72, 8, 128], P(None, 'elem', 'band'), may hold values from -6 to 6
- kappa: float32 [8, 128], P('elem', 'band'), may hold values from 0.02 to 0.2
- substeps: int32 [8, 128], P('elem', 'band'), may hold values from 1 to 4, as said below
- coupling: float32 [6, 6], replicated, may hold values from -2.5 to 2.5
- level_map: float32 [60, 72], replicated, may hold values from -0.75 to 0.75
- field_scale: float32 [6], replicated, may hold values from 0.5 to 1.5
- back_map: float32 [72, 60], replicated, may hold values from -0.75 to 0.75
- back_weight: float32 [6], replicated, may hold values from -3 to 3
Outputs:
- crm_final: bfloat16 [8, 128, 6, 3840], P('elem', 'band')
- host_final: float32 [72, 8, 128], P(None, 'elem', 'band')
The draws below stay inside these ranges and needn't reach their ends.
Inputs may be any that keep to these rules, and one draw needn't show every extreme that they name: Each aligned block of 1 x 32 columns (the columns of one device) draws a level from 1 to 4; each column of the block takes 1 plus a uniform integer modulo that level substeps. Column (0, 0) takes 4 substeps and column (0, 1) takes 1.
All inputs are finite; a program needn't handle non-finite values.
Results may differ from the reference program's by a relative error of at most 0.0055.
Values may be sent and summed in bfloat16 or wider, within the bound.
No kernel may reach another device: no remote copies, remote signals or barrier semaphores. Data moves between devices by JAX's collectives and lax.ppermute only.
A program may use at most 128 MiB of HBM per device.

```python
import math
import jax
import jax.numpy as jnp
from jax import lax

LEV = 72
FIELDS = 6
NZC = 60
NXC = 64
SUB = 4
WINDOWS = 2
CXH = 1
CYH = 32
NGX = 8
NGY = 128


def draw_substeps(key, part):
    first_key, second_key = jax.random.split(jax.random.fold_in(key, 17))
    level = jax.random.randint(first_key, (NGX // CXH, NGY // CYH), 1, SUB + 1)
    level = jnp.repeat(jnp.repeat(level, CXH, axis=0), CYH, axis=1)
    raw = jax.random.randint(second_key, (NGX, NGY), 0, 1048576)
    counts = 1 + raw % level
    counts = counts.at[0, 0].set(SUB)
    counts = counts.at[0, 1].set(1)
    return counts.astype(jnp.int32)


def block_scale(rng, shape, shards, least, high):
    def one(axis_at, shards_of):
        draws = jax.random.uniform(jax.random.fold_in(jax.random.fold_in(rng, 6), axis_at), (shards_of,), jnp.float32, least / len(shards), high / len(shards))
        return jnp.repeat(jnp.exp(draws), shape[axis_at] // shards_of).reshape((-1,) + (1,) * (len(shape) - axis_at - 1))

    loudness = one(*shards[0])
    for cut in shards[1:]:
        loudness = loudness * one(*cut)
    return loudness


def normal_values(stream_key, dims, width, most, pieces=(), held_as=jnp.bfloat16):
    values = width * jax.random.normal(stream_key, dims, jnp.float32)
    if pieces:
        values = values * block_scale(stream_key, dims, pieces, -0.22, 0.18)
    return jnp.clip(values, -most, most).astype(held_as)


def setup_inputs(seed: int = 0) -> dict:
    keys = jax.random.split(jax.random.key(seed), 10)
    crm_state = normal_values(keys[0], (NGX, NGY, FIELDS, NZC * NXC), 1.0, 6.0, ((0, 8), (1, 4)))
    host_state = normal_values(keys[1], (LEV, NGX, NGY), 1.0, 6.0, ((1, 8), (2, 4)), jnp.float32)
    kappa = jnp.clip(jnp.exp(math.log(0.2) - 2.3025851 * jax.random.uniform(keys[2], (NGX, NGY), jnp.float32) ** block_scale(keys[2], (NGX, NGY), ((0, 8), (1, 4)), -0.2, 0.2)), 0.02, 0.2)
    substeps = draw_substeps(jax.random.fold_in(keys[9], 71), 0)
    coupling = normal_values(keys[4], (FIELDS, FIELDS), FIELDS ** -0.5, 2.5, (), jnp.float32)
    level_map = normal_values(keys[5], (NZC, LEV), LEV ** -0.5, 0.75, (), jnp.float32)
    field_scale = jnp.clip(jax.random.uniform(keys[6], (FIELDS,), jnp.float32, 0.5, 1.5), 0.5, 1.5)
    back_map = normal_values(keys[7], (LEV, NZC), NZC ** -0.5, 0.75, (), jnp.float32)
    back_weight = normal_values(keys[8], (FIELDS,), 1.0, 3.0, (), jnp.float32)
    return dict(crm_state=crm_state, host_state=host_state, kappa=kappa, substeps=substeps, coupling=coupling, level_map=level_map, field_scale=field_scale, back_map=back_map, back_weight=back_weight)


cloud_step = 0.1
return_scale = 1.0


def cloud_substep(fields, forcing, coupling, active):
    highest = lax.Precision.HIGHEST
    wind = fields[:, 0]
    deriv = 0.5 * (jnp.roll(fields, -1, axis=3) - jnp.roll(fields, 1, axis=3))
    padded = jnp.pad(fields, ((0, 0), (0, 0), (1, 1), (0, 0)))
    vertical = padded[:, :, 2:] - 2.0 * fields + padded[:, :, :-2]
    mixing = jnp.tanh(jnp.einsum('fg,ngzx->nfzx', coupling, fields, precision=highest))
    change = cloud_step * (-wind[:, None] * deriv + vertical + mixing + forcing[..., None])
    return fields + jnp.where(active[:, None, None, None], change, 0.0)


def host_section(host, tend, kappa):
    def face(host_near, kappa_near):
        return 0.5 * (kappa + kappa_near) * (host_near - host)
    spread = face(jnp.roll(host, -1, 1), jnp.roll(kappa, -1, 0)) + face(jnp.roll(host, 1, 1), jnp.roll(kappa, 1, 0))
    spread = spread + face(jnp.roll(host, -1, 2), jnp.roll(kappa, -1, 1)) + face(jnp.roll(host, 1, 2), jnp.roll(kappa, 1, 1))
    return host + (tend + spread)


def reference(crm_state, host_state, kappa, substeps, coupling, level_map, field_scale, back_map, back_weight):
    highest = lax.Precision.HIGHEST
    cloud = crm_state.astype(jnp.float32).reshape(NGX, NGY, FIELDS, NZC, NXC)
    host = host_state
    for window in range(WINDOWS):
        columns = jnp.transpose(host, (1, 2, 0))

        def run_row(items):
            fields, column_row, counts = items
            mapped = jnp.einsum('zl,nl->nz', level_map, column_row, precision=highest)
            forcing = field_scale[None, :, None] * mapped[:, None, :]
            start = fields
            for turn in range(SUB):
                fields = cloud_substep(fields, forcing, coupling, counts > turn)
            mean = jnp.mean(fields - start, axis=-1)
            mixed = jnp.einsum('f,nfz->nz', back_weight, mean, precision=highest)
            tend = return_scale * jnp.einsum('lz,nz->nl', back_map, mixed, precision=highest)
            return fields, tend

        cloud, tend = lax.map(run_row, (cloud, columns, substeps))
        host = host_section(host, jnp.transpose(tend, (2, 0, 1)), kappa)
    crm_final = cloud.reshape(NGX, NGY, FIELDS, NZC * NXC).astype(jnp.bfloat16)
    return crm_final, host
```

```python
import jax
import jax.numpy as jnp
from jax import lax
from jax.experimental import pallas as pl
from jax.experimental.pallas import tpu as pltpu
from jax.sharding import PartitionSpec as P

FIELDS = 6
NZC = 60
NXC = 64
SUB = 4
LANES = 2 * NXC
COLS = 32
SIZE = 8
GROUPS = COLS // SIZE
QUARTER = NZC // 4
TILES = NZC // 2
CLOUD_STEP = 0.1
F32 = jnp.float32
BF16 = jnp.bfloat16


def lane_iota(rows, lanes=LANES):
    return lax.broadcasted_iota(jnp.int32, (rows, lanes), 1)


def row_iota(rows, lanes):
    return lax.broadcasted_iota(jnp.int32, (rows, lanes), 0)


def ranks(counts_row):
    rows = row_iota(COLS, COLS)
    lanes = lane_iota(COLS, COLS)
    along_lanes = jnp.broadcast_to(counts_row, (COLS, COLS))
    eye = rows == lanes
    column = jnp.sum(jnp.where(eye, along_lanes, 0.0), axis=1, keepdims=True)
    along_rows = jnp.broadcast_to(column, (COLS, COLS))
    before = (along_lanes > along_rows) | ((along_lanes == along_rows) & (lanes < rows))
    rank_col = jnp.sum(jnp.where(before, 1.0, 0.0), axis=1, keepdims=True)
    after = (along_rows > along_lanes) | ((along_rows == along_lanes) & (rows < lanes))
    rank_row = jnp.sum(jnp.where(after, 1.0, 0.0), axis=0, keepdims=True)
    to_slot = jnp.where(jnp.broadcast_to(rank_row, (COLS, COLS)) == rows.astype(F32), 1.0, 0.0)
    to_column = jnp.where(jnp.broadcast_to(rank_col, (COLS, COLS)) == lanes.astype(F32), 1.0, 0.0)
    return to_slot, to_column, column


def hi_lo(value):
    hi = value.astype(BF16)
    rest = value - hi.astype(F32)
    mid = rest.astype(BF16)
    return hi, mid, (rest - mid.astype(F32)).astype(BF16)


def permuted(matrix, value):
    one_hot = matrix.astype(BF16)
    total = None
    for part in hi_lo(value):
        term = jnp.dot(one_hot, part, preferred_element_type=F32)
        total = term if total is None else total + term
    return total


def block_diagonal(matrix):
    wide = jnp.concatenate([matrix] * FIELDS, axis=1)
    tall = jnp.concatenate([wide] * FIELDS, axis=0)
    size = FIELDS * COLS
    same = row_iota(size, size) // COLS == lane_iota(size, size) // COLS
    return jnp.where(same, tall, 0.0).astype(BF16)


def quarter_of(level):
    part, place = divmod(level, QUARTER)
    half, sub = divmod(part, 2)
    return half, sub, place


def weighted(state, g, zi, weights):
    total = weights[0] * state[g, zi, 0]
    for f in range(1, FIELDS):
        total = total + weights[f] * state[g, zi, f]
    return total


def run_window(
    state, sums, fresh_sums, host_sorted, counts_sorted, most, coup, level_t, back_t, fscale, bweight,
    cells, force, splat, tend_sorted,
):
    lanes8 = lane_iota(SIZE)
    low8 = lanes8 < NXC
    for f in range(FIELDS):
        for g in range(FIELDS):
            splat[f, g] = jnp.full((2 * SIZE, LANES), coup[f, g], F32).astype(BF16)
    mapped_all = jnp.dot(
        host_sorted, level_t, precision=lax.Precision.HIGHEST, preferred_element_type=F32
    )
    lanes16 = lax.broadcasted_iota(jnp.int32, (2 * SIZE, LANES), 1)
    at_end = (lanes16 % NXC) == NXC - 1
    at_start = (lanes16 % NXC) == 0
    weights = [bweight[f] for f in range(FIELDS)]
    ones_rows = row_iota(LANES, 2 * LANES)
    ones_lanes = lane_iota(LANES, 2 * LANES)
    averager = jnp.where(ones_rows // NXC == ones_lanes // LANES, 1.0 / NXC, 0.0).astype(BF16)

    for g in range(GROUPS):
        mapped = mapped_all[g * SIZE : (g + 1) * SIZE, :]
        for zi in range(QUARTER):
            rows = []
            for sub in range(2):
                low = mapped[:, sub * QUARTER + zi : sub * QUARTER + zi + 1]
                high = mapped[:, (2 + sub) * QUARTER + zi : (2 + sub) * QUARTER + zi + 1]
                rows.append(
                    jnp.where(
                        low8,
                        jnp.broadcast_to(low, (SIZE, LANES)),
                        jnp.broadcast_to(high, (SIZE, LANES)),
                    )
                )
            spread = jnp.concatenate(rows, axis=0)
            for f in range(FIELDS):
                force[zi, f] = (fscale[f] * spread).astype(BF16)
                cells[0, zi, f] = state[g, zi, f].astype(BF16)
            if fresh_sums:
                sums[g, zi] = weighted(state, g, zi, weights)
        count_here = counts_sorted[g * SIZE : (g + 1) * SIZE, :]
        count_full = jnp.broadcast_to(
            jnp.concatenate([count_here, count_here], axis=0), (2 * SIZE, LANES)
        )

        def substep(turn, carry, g=g, count_full=count_full):
            src = lax.rem(turn, 2)
            dst = 1 - src
            step = jnp.where(count_full > turn.astype(F32), CLOUD_STEP, 0.0).astype(BF16)
            below = []
            above = []
            for f in range(FIELDS):
                first = state[g, 0, f]
                last = state[g, QUARTER - 1, f]
                above.append(
                    jnp.concatenate(
                        [
                            first[SIZE:],
                            jnp.where(low8, pltpu.roll(first[:SIZE], NXC, 1), 0.0),
                        ],
                        axis=0,
                    ).astype(BF16)
                )
                below.append(
                    jnp.concatenate(
                        [
                            jnp.where(low8, 0.0, pltpu.roll(last[SIZE:], NXC, 1)),
                            last[:SIZE],
                        ],
                        axis=0,
                    ).astype(BF16)
                )
            for zi in range(QUARTER):
                now = [cells[src, zi, f] for f in range(FIELDS)]
                prev = below if zi == 0 else [cells[src, zi - 1, f] for f in range(FIELDS)]
                after = (
                    above if zi == QUARTER - 1 else [cells[src, zi + 1, f] for f in range(FIELDS)]
                )
                wind = now[0] * jnp.asarray(-0.5, BF16)
                for f in range(FIELDS):
                    here = now[f]
                    plus = jnp.where(
                        at_end, pltpu.roll(here, NXC - 1, 1), pltpu.roll(here, LANES - 1, 1)
                    )
                    minus = jnp.where(at_start, pltpu.roll(here, NXC + 1, 1), pltpu.roll(here, 1, 1))
                    mix = splat[f, 0] * now[0]
                    for other in range(1, FIELDS):
                        mix = mix + splat[f, other] * now[other]
                    change = (prev[f] + after[f]) - (here + here)
                    change = change + wind * (plus - minus)
                    change = change + jnp.tanh(mix) + force[zi, f]
                    new = state[g, zi, f] + (step * change).astype(F32)
                    state[g, zi, f] = new
                    cells[dst, zi, f] = new.astype(BF16)
            return carry

        lax.fori_loop(0, most[g], substep, 0)

        total = jnp.zeros((2 * SIZE, LANES), F32)
        for zi in range(QUARTER):
            end = weighted(state, g, zi, weights)
            diff = end - sums[g, zi]
            sums[g, zi] = end
            hi = diff.astype(BF16)
            lo = (diff - hi.astype(F32)).astype(BF16)
            mean = jnp.dot(hi, averager, preferred_element_type=F32) + jnp.dot(
                lo, averager, preferred_element_type=F32
            )
            for half in range(2):
                first = 2 * half * QUARTER + zi
                second = first + QUARTER
                back = jnp.concatenate(
                    [
                        jnp.broadcast_to(back_t[first : first + 1, :], (SIZE, LANES)),
                        jnp.broadcast_to(back_t[second : second + 1, :], (SIZE, LANES)),
                    ],
                    axis=0,
                )
                total = total + mean[:, half * LANES : (half + 1) * LANES] * back
        tend_sorted[g * SIZE : (g + 1) * SIZE, :] = total[:SIZE] + total[SIZE:]


def group_most(counts_row):
    most = []
    over = [jnp.sum(jnp.where(counts_row > turn, 1, 0)) for turn in range(1, SUB)]
    for g in range(GROUPS):
        most.append(1 + sum(jnp.where(over_turn > g * SIZE, 1, 0) for over_turn in over))
    return most


def first_kernel(
    cloud, host, counts, coup, level_t, back_t, fscale, bweight, state, sums, tend,
    cells, force, splat, tend_sorted, natural,
):
    counts_row = counts[...]
    to_slot, to_column, column = ranks(counts_row.astype(F32))
    most = group_most(counts_row)
    block = block_diagonal(to_slot)
    low = lane_iota(SIZE) < NXC
    for tile in range(TILES // 2):
        lanes = slice(tile * LANES, (tile + 1) * LANES)
        lanes_far = slice((tile + TILES // 2) * LANES, (tile + TILES // 2 + 1) * LANES)
        near = cloud[:, :, lanes].reshape(FIELDS * COLS, LANES)
        far = cloud[:, :, lanes_far].reshape(FIELDS * COLS, LANES)
        both = jnp.dot(
            block, jnp.concatenate([near, far], axis=1), preferred_element_type=F32
        )
        near = both[:, :LANES]
        far = both[:, LANES:]
        even = jnp.where(low, 1.0, 0.0)
        for parity in range(2):
            half, sub, place = quarter_of(2 * tile + parity)
            for f in range(FIELDS):
                for g in range(GROUPS):
                    row = f * COLS + g * SIZE
                    a = near[row : row + SIZE]
                    b = far[row : row + SIZE]
                    if parity == 0:
                        value = jnp.where(low, a, pltpu.roll(b, NXC, 1))
                    else:
                        value = jnp.where(low, pltpu.roll(a, NXC, 1), b)
                    state[g, place, f, sub * SIZE : (sub + 1) * SIZE, :] = value
    counts_sorted = permuted(to_slot, jnp.broadcast_to(column, (COLS, LANES)))
    run_window(
        state, sums, True, permuted(to_slot, host[...]), counts_sorted, most, coup, level_t[...],
        back_t, fscale, bweight, cells, force, splat, tend_sorted,
    )
    tend[...] = permuted(to_column, tend_sorted[...])


def second_kernel(
    state_in, sums_in, host, counts, coup, level_t, back_t, fscale, bweight, cloud_out, tend,
    state, sums, cells, force, splat, tend_sorted, natural,
):
    counts_row = counts[...]
    to_slot, to_column, column = ranks(counts_row.astype(F32))
    most = group_most(counts_row)
    counts_sorted = permuted(to_slot, jnp.broadcast_to(column, (COLS, LANES)))
    for g in range(GROUPS):
        for zi in range(QUARTER):
            sums[g, zi] = sums_in[g, zi]
            for f in range(FIELDS):
                state[g, zi, f] = state_in[g, zi, f]
    run_window(
        state, sums, False, permuted(to_slot, host[...]), counts_sorted, most, coup, level_t[...],
        back_t, fscale, bweight, cells, force, splat, tend_sorted,
    )
    tend[...] = permuted(to_column, tend_sorted[...])
    block = block_diagonal(to_column)
    low = lane_iota(SIZE) < NXC
    for tile in range(TILES):
        lanes = slice(tile * LANES, (tile + 1) * LANES)
        half, sub, place = quarter_of(2 * tile)
        half2, sub2, place2 = quarter_of(2 * tile + 1)
        rows = []
        for f in range(FIELDS):
            for g in range(GROUPS):
                a = state[g, place, f, sub * SIZE : (sub + 1) * SIZE, :]
                b = state[g, place2, f, sub2 * SIZE : (sub2 + 1) * SIZE, :]
                if half == 0:
                    b = pltpu.roll(b, NXC, 1)
                else:
                    a = pltpu.roll(a, NXC, 1)
                rows.append(jnp.where(low, a, b))
        stacked = jnp.concatenate(rows, axis=0).astype(BF16)
        out = jnp.dot(block, stacked, preferred_element_type=F32).astype(BF16)
        cloud_out[:, :, lanes] = out.reshape(FIELDS, COLS, LANES)


def host_kernel(host, kappa, tend, east_h, west_h, north_h, south_h, east_k, west_k, north_k, south_k, out):
    centre = host[...]
    mid = kappa[...]

    def face(near, near_k):
        return 0.5 * (mid + near_k) * (near - centre)

    spread = face(east_h[...], east_k[...]) + face(west_h[...], west_k[...])
    up_h = jnp.concatenate([centre[1:], north_h[0:1]], axis=0)
    up_k = jnp.concatenate([mid[1:], north_k[0:1]], axis=0)
    down_h = jnp.concatenate([south_h[COLS - 1 : COLS], centre[:-1]], axis=0)
    down_k = jnp.concatenate([south_k[COLS - 1 : COLS], mid[:-1]], axis=0)
    spread = spread + face(up_h, up_k) + face(down_h, down_k)
    out[...] = centre + (tend[:, : centre.shape[1]] + spread)


def neighbours(block):
    found = []
    for axis in ("elem", "band"):
        count = lax.axis_size(axis)
        forward = [(i, (i + 1) % count) for i in range(count)]
        backward = [(target, source) for source, target in forward]
        found.append(lax.ppermute(block, axis, backward))
        found.append(lax.ppermute(block, axis, forward))
    return found


VMEM = pl.BlockSpec(memory_space=pltpu.VMEM)
SMEM = pl.BlockSpec(memory_space=pltpu.SMEM)
PARAMS = pltpu.CompilerParams(vmem_limit_bytes=56 * 1024 * 1024)


def body(
    crm_state, host_state, kappa, substeps, coupling, level_map, field_scale, back_map, back_weight
):
    levels = host_state.shape[0]
    cloud = jnp.transpose(crm_state[0], (1, 0, 2))
    host = jnp.transpose(host_state[:, 0, :], (1, 0))
    kap = jnp.broadcast_to(kappa.reshape(COLS, 1), (COLS, LANES))
    level_t = level_map.T
    back_t = jnp.pad(back_map.T, ((0, 0), (0, LANES - levels)))
    state_shape = jax.ShapeDtypeStruct((GROUPS, QUARTER, FIELDS, 2 * SIZE, LANES), F32)
    sums_shape = jax.ShapeDtypeStruct((GROUPS, QUARTER, 2 * SIZE, LANES), F32)
    tend_shape = jax.ShapeDtypeStruct((COLS, LANES), F32)
    scratch = [
        pltpu.VMEM((2, QUARTER, FIELDS, 2 * SIZE, LANES), BF16),
        pltpu.VMEM((QUARTER, FIELDS, 2 * SIZE, LANES), BF16),
        pltpu.VMEM((FIELDS, FIELDS, 2 * SIZE, LANES), BF16),
        pltpu.VMEM((COLS, LANES), F32),
        pltpu.VMEM((FIELDS, COLS, LANES), BF16),
    ]
    weights = (coupling, level_t, back_t, field_scale, back_weight)
    weight_specs = [SMEM, VMEM, VMEM, SMEM, SMEM]

    kap_near = neighbours(kap)
    host_near = neighbours(host)
    state, sums, tend = pl.pallas_call(
        first_kernel,
        out_shape=(state_shape, sums_shape, tend_shape),
        in_specs=[VMEM, VMEM, VMEM] + weight_specs,
        out_specs=(VMEM, VMEM, VMEM),
        scratch_shapes=scratch,
        compiler_params=PARAMS,
        name="first_window",
    )(cloud, host, substeps, *weights)

    def advance(host, tend, near):
        return pl.pallas_call(
            host_kernel,
            out_shape=jax.ShapeDtypeStruct((COLS, levels), F32),
            in_specs=[VMEM] * 11,
            out_specs=VMEM,
            name="host_section",
        )(host, kap[:, :1], tend, *near, *[k[:, :1] for k in kap_near])

    host = advance(host, tend, host_near)
    host_near = neighbours(host)
    cloud_out, tend = pl.pallas_call(
        second_kernel,
        out_shape=(jax.ShapeDtypeStruct(cloud.shape, BF16), tend_shape),
        in_specs=[VMEM, VMEM, VMEM, VMEM] + weight_specs,
        out_specs=(VMEM, VMEM),
        scratch_shapes=[
            pltpu.VMEM(state_shape.shape, F32),
            pltpu.VMEM(sums_shape.shape, F32),
        ]
        + scratch,
        compiler_params=PARAMS,
        name="second_window",
    )(state, sums, host, substeps, *weights)
    host = advance(host, tend, host_near)
    crm_final = jnp.transpose(cloud_out, (1, 0, 2))[None]
    host_final = jnp.transpose(host, (1, 0))[:, None, :]
    return (crm_final, host_final)


def solution(mesh):
    return jax.shard_map(
        body,
        mesh=mesh,
        in_specs=(
            P("elem", "band", None, None),
            P(None, "elem", "band"),
            P("elem", "band"),
            P("elem", "band"),
            P(),
            P(),
            P(),
            P(),
            P(),
        ),
        out_specs=(P("elem", "band", None, None), P(None, "elem", "band")),
        check_vma=False,
    )
```

```python
import jax
import jax.numpy as jnp
from jax import lax
from jax.experimental import pallas as pl
from jax.experimental.pallas import tpu as pltpu
from jax.sharding import PartitionSpec as P

FIELDS = 6
NZC = 60
NXC = 64
SUB = 4
WINDOWS = 2
LANES = 2 * NXC
COLS = 32
SIZE = 8
PAIR = 2 * SIZE
GROUPS = COLS // SIZE
QUARTER = NZC // 4
HALF_TILES = NZC // 4
CELLS = NZC * NXC
CHUNK = 3
CLOUD_STEP = 0.1
F32 = jnp.float32
BF16 = jnp.bfloat16
HIGHEST = lax.Precision.HIGHEST


def row_iota(*shape):
    return lax.broadcasted_iota(jnp.int32, shape, 0)


def lane_iota(*shape):
    return lax.broadcasted_iota(jnp.int32, shape, 1)


def column_of(row):
    square = jnp.broadcast_to(row, (COLS, COLS))
    eye = row_iota(COLS, COLS) == lane_iota(COLS, COLS)
    return jnp.sum(jnp.where(eye, square, 0.0), axis=1, keepdims=True)


def ranks(counts_row):
    rows = row_iota(COLS, COLS)
    lanes = lane_iota(COLS, COLS)
    along_lanes = jnp.broadcast_to(counts_row, (COLS, COLS))
    column = column_of(counts_row)
    along_rows = jnp.broadcast_to(column, (COLS, COLS))
    before = (along_lanes > along_rows) | ((along_lanes == along_rows) & (lanes < rows))
    rank_col = jnp.sum(jnp.where(before, 1.0, 0.0), axis=1, keepdims=True)
    after = (along_rows > along_lanes) | ((along_rows == along_lanes) & (rows < lanes))
    rank_row = jnp.sum(jnp.where(after, 1.0, 0.0), axis=0, keepdims=True)
    to_slot = jnp.where(jnp.broadcast_to(rank_row, (COLS, COLS)) == rows.astype(F32), 1.0, 0.0)
    to_column = jnp.where(jnp.broadcast_to(rank_col, (COLS, COLS)) == lanes.astype(F32), 1.0, 0.0)
    return to_slot, to_column, column


def hi_lo(value):
    hi = value.astype(BF16)
    rest = value - hi.astype(F32)
    mid = rest.astype(BF16)
    return hi, mid, (rest - mid.astype(F32)).astype(BF16)


def permuted(one_hot, value):
    total = None
    for part in hi_lo(value):
        term = jnp.dot(one_hot, part, preferred_element_type=F32)
        total = term if total is None else total + term
    return total


def quarter_of(level):
    part, place = divmod(level, QUARTER)
    half, sub = divmod(part, 2)
    return half, sub, place


def weighted(state, g, zi, weights):
    total = weights[0] * state[g, zi, 0]
    for f in range(1, FIELDS):
        total = total + weights[f] * state[g, zi, f]
    return total


def prepare_force(force, host_sorted, level_map, fscale, expand):
    mapped = lax.dot_general(
        host_sorted, level_map[...], (((1,), (1,)), ((), ())), precision=HIGHEST,
        preferred_element_type=F32,
    )
    mapped = jnp.concatenate([mapped, jnp.zeros((COLS, NXC - NZC), F32)], axis=1)
    hi = mapped.astype(BF16)
    lo = (mapped - hi.astype(F32)).astype(BF16)
    parts = jnp.concatenate([hi, lo], axis=0)
    for zi in range(QUARTER):
        both = jnp.dot(
            parts, expand[:, 2 * zi * LANES : 2 * (zi + 1) * LANES], preferred_element_type=F32
        )
        both = both[:COLS] + both[COLS:]
        for g in range(GROUPS):
            rows = both[g * SIZE : (g + 1) * SIZE]
            spread = jnp.concatenate([rows[:, :LANES], rows[:, LANES:]], axis=0)
            for f in range(FIELDS):
                force[g, zi, f] = fscale[f] * spread


def advance_window(state, force, counts16, most, edge, dmat, cmat):
    low = lane_iota(SIZE, LANES) < NXC

    def substep(turn, active):
        for g in range(active):
            step = jnp.where(counts16[g] > turn.astype(F32), CLOUD_STEP, 0.0)
            keep = 1.0 - 2.0 * step
            prev = []
            for f in range(FIELDS):
                first = state[g, 0, f]
                last = state[g, QUARTER - 1, f]
                edge[g, f] = jnp.concatenate(
                    [first[SIZE:], jnp.where(low, pltpu.roll(first[:SIZE], NXC, 1), 0.0)], axis=0
                )
                prev.append(
                    jnp.concatenate(
                        [jnp.where(low, 0.0, pltpu.roll(last[SIZE:], NXC, 1)), last[:SIZE]], axis=0
                    )
                )
            for start in range(0, QUARTER, CHUNK):
                places = range(start, start + CHUNK)
                flats = [state[g, zi].reshape(FIELDS * PAIR, LANES).astype(BF16) for zi in places]
                slopes = jnp.dot(
                    jnp.concatenate(flats, axis=0), dmat[...], preferred_element_type=F32
                )
                for i, zi in enumerate(places):
                    mixed = jnp.dot(cmat[...], flats[i], preferred_element_type=F32)
                    now = [state[g, zi, f] for f in range(FIELDS)]
                    news = []
                    for f in range(FIELDS):
                        rows = slice(f * PAIR, (f + 1) * PAIR)
                        here = (i * FIELDS + f) * PAIR
                        slope = slopes[here : here + PAIR]
                        after = edge[g, f] if zi == QUARTER - 1 else state[g, zi + 1, f]
                        change = (prev[f] + after) + (
                            now[0] * slope + (jnp.tanh(mixed[rows]) + force[g, zi, f])
                        )
                        news.append(keep * now[f] + step * change)
                    for f in range(FIELDS):
                        state[g, zi, f] = news[f]
                    prev = now

    def body(turn, carry):
        running = sum(jnp.where(most[g] > turn, 1, 0) for g in range(GROUPS))
        for active in range(1, GROUPS + 1):
            pl.when(running == active)(lambda active=active: substep(turn, active))
        return carry

    lax.fori_loop(0, most[0], body, 0)


def differences(state, sums, weights, diffs):
    for zi in range(QUARTER):
        changes = []
        for g in range(GROUPS):
            end = weighted(state, g, zi, weights)
            changes.append(end - sums[g, zi])
            sums[g, zi] = end
        for sub in range(2):
            rows = jnp.concatenate([c[sub * SIZE : (sub + 1) * SIZE] for c in changes], axis=0)
            place = 2 * zi + sub
            diffs[:, place * LANES : (place + 1) * LANES] = rows.astype(BF16)


def tendency(diffs, backx, to_column):
    both = jnp.dot(diffs[...], backx[...], preferred_element_type=F32)
    return permuted(to_column, both[:, :LANES] + both[:, LANES:])


def swapped_halves(low, one, two):
    outer = jnp.where(low, one, two)
    inner = pltpu.roll(jnp.where(low, two, one), NXC, 1)
    return jnp.where(low, outer, inner), jnp.where(low, inner, outer)


def cloud_kernel(
    cloud_in, own_in, east_in, west_in, north_in, south_in, counts_in, level_in, back_in, coup_in, fscale_in,
    bweight_in,
    cloud_out, host_out, aux_out,
    own, east, west, north, south, counts, level_map, back_t, coup, fscale, bweight,
    state, force, sums, edge, dmat, cmat, counts16, backx, diffs, most, expand,
    out_buf, cloud, host_buf, aux, sems,
):
    levels = host_out.shape[1]
    sources = (
        own_in, east_in, west_in, north_in, south_in, counts_in, level_in, back_in, coup_in, fscale_in,
        bweight_in,
    )
    places = (own, east, west, north, south, counts, level_map, back_t, coup, fscale, bweight)
    copies = [
        pltpu.make_async_copy(src, dst, sems.at[FIELDS + i])
        for i, (src, dst) in enumerate(zip(sources, places))
    ]
    for copy in copies:
        copy.start()
    loads = [
        pltpu.make_async_copy(cloud_in.at[f], cloud.at[f], sems.at[f]) for f in range(FIELDS)
    ]
    for copy in loads:
        copy.start()
    r, l = row_iota(LANES, LANES), lane_iota(LANES, LANES)
    same = (r // NXC) == (l // NXC)
    ahead = same & (r % NXC == (l + 1) % NXC)
    behind = same & (r % NXC == (l + NXC - 1) % NXC)
    dmat[...] = (jnp.where(behind, 0.5, 0.0) - jnp.where(ahead, 0.5, 0.0)).astype(BF16)
    r, l = row_iota(NXC, LANES), lane_iota(NXC, LANES)
    for zi in range(QUARTER):
        for sub in range(2):
            level = sub * QUARTER + zi
            level = jnp.where(l < NXC, level, level + 2 * QUARTER)
            part = slice((2 * zi + sub) * LANES, (2 * zi + sub + 1) * LANES)
            expand[:, part] = jnp.where(r == level, 1.0, 0.0).astype(BF16)
    for copy in copies:
        copy.wait()

    counts_row = counts[...].astype(F32)
    to_slot, to_column, column = ranks(counts_row)
    to_slot = to_slot.astype(BF16)
    to_column = to_column.astype(BF16)
    over = [jnp.sum(jnp.where(counts[...] > turn, 1, 0)) for turn in range(1, SUB)]
    for g in range(GROUPS):
        most[g] = 1 + sum(jnp.where(over_turn > g * SIZE, 1, 0) for over_turn in over)
    counts_sorted = jnp.dot(
        to_slot, jnp.broadcast_to(column, (COLS, LANES)).astype(BF16), preferred_element_type=F32
    )
    for g in range(GROUPS):
        rows = counts_sorted[g * SIZE : (g + 1) * SIZE]
        counts16[g] = jnp.concatenate([rows, rows], axis=0)
    weights = [bweight[f] for f in range(FIELDS)]

    r, l = row_iota(FIELDS * PAIR, FIELDS * PAIR), lane_iota(FIELDS * PAIR, FIELDS * PAIR)
    same = (r % PAIR) == (l % PAIR)
    mixer = jnp.zeros((FIELDS * PAIR, FIELDS * PAIR), F32)
    for f in range(FIELDS):
        for other in range(FIELDS):
            here = same & (r // PAIR == f) & (l // PAIR == other)
            mixer = jnp.where(here, coup[f, other], mixer)
    cmat[...] = mixer.astype(BF16)
    padding = jnp.zeros((1, LANES - levels), F32)
    for zi in range(QUARTER):
        for sub in range(2):
            for half in range(2):
                level = (2 * half + sub) * QUARTER + zi
                row = jnp.concatenate([back_t[level : level + 1, :], padding], axis=1) * (1.0 / NXC)
                hi = row.astype(BF16)
                lo = (row - hi.astype(F32)).astype(BF16)
                first = ((2 * zi + sub) * 2 + half) * NXC
                backx[first : first + NXC, :LANES] = jnp.broadcast_to(hi, (NXC, LANES))
                backx[first : first + NXC, LANES:] = jnp.broadcast_to(lo, (NXC, LANES))

    host = own[:COLS]
    kap, kap_e, kap_w, kap_n, kap_s = (
        column_of(ref[COLS : COLS + 1, :COLS]) for ref in (own, east, west, north, south)
    )
    face_e = 0.5 * (kap + kap_e)
    face_w = 0.5 * (kap + kap_w)
    face_n = 0.5 * (kap + jnp.concatenate([kap[1:], kap_n[:1]], axis=0))
    face_s = 0.5 * (kap + jnp.concatenate([kap_s[COLS - 1 :], kap[:-1]], axis=0))
    spread = face_e * (east[:COLS] - host) + face_w * (west[:COLS] - host)
    spread = spread + face_n * (jnp.concatenate([host[1:], north[0:1]], axis=0) - host)
    spread = spread + face_s * (
        jnp.concatenate([south[COLS - 1 : COLS], host[:-1]], axis=0) - host
    )

    prepare_force(force, permuted(to_slot, host), level_map, fscale, expand)

    low = lane_iota(SIZE, LANES) < NXC
    for copy in loads:
        copy.wait()
    for f in range(FIELDS):
        for tile in range(HALF_TILES):
            near = slice(tile * LANES, (tile + 1) * LANES)
            far = slice((tile + HALF_TILES) * LANES, (tile + HALF_TILES + 1) * LANES)
            _, sub, place = quarter_of(2 * tile)
            _, sub2, place2 = quarter_of(2 * tile + 1)
            both = jnp.dot(
                to_slot, jnp.concatenate([cloud[f, :, near], cloud[f, :, far]], axis=1),
                preferred_element_type=F32,
            )
            for g in range(GROUPS):
                rows = both[g * SIZE : (g + 1) * SIZE]
                even, odd = swapped_halves(low, rows[:, :LANES], rows[:, LANES:])
                state[g, place, f, sub * SIZE : (sub + 1) * SIZE, :] = even
                state[g, place2, f, sub2 * SIZE : (sub2 + 1) * SIZE, :] = odd
    for g in range(GROUPS):
        for zi in range(QUARTER):
            sums[g, zi] = weighted(state, g, zi, weights)

    advance_window(state, force, counts16, most, edge, dmat, cmat)
    differences(state, sums, weights, diffs)
    tend = tendency(diffs, backx, to_column)
    host = host + (tend[:, :levels] + spread)
    host_buf[...] = host
    sending = [pltpu.make_async_copy(host_buf, host_out, sems.at[0])]
    sending[0].start()
    prepare_force(force, permuted(to_slot, host), level_map, fscale, expand)
    advance_window(state, force, counts16, most, edge, dmat, cmat)
    differences(state, sums, weights, diffs)
    for tile in range(HALF_TILES):
        near = slice(tile * LANES, (tile + 1) * LANES)
        far = slice((tile + HALF_TILES) * LANES, (tile + HALF_TILES + 1) * LANES)
        _, sub, place = quarter_of(2 * tile)
        _, sub2, place2 = quarter_of(2 * tile + 1)
        for f in range(FIELDS):
            near_rows = []
            far_rows = []
            for g in range(GROUPS):
                even = state[g, place, f, sub * SIZE : (sub + 1) * SIZE, :]
                odd = state[g, place2, f, sub2 * SIZE : (sub2 + 1) * SIZE, :]
                one, two = swapped_halves(low, even, odd)
                near_rows.append(one)
                far_rows.append(two)
            rows = jnp.concatenate(
                [jnp.concatenate(near_rows, axis=0), jnp.concatenate(far_rows, axis=0)], axis=1
            )
            out = jnp.dot(to_column, rows.astype(BF16), preferred_element_type=F32)
            out_buf[f, :, near] = out[:, :LANES].astype(BF16)
            out_buf[f, :, far] = out[:, LANES:].astype(BF16)
    for f in range(FIELDS):
        copy = pltpu.make_async_copy(out_buf.at[f], cloud_out.at[f], sems.at[len(sending)])
        copy.start()
        sending.append(copy)

    tend = tendency(diffs, backx, to_column)
    zero = jnp.zeros((1, levels), F32)
    base = host + (tend[:, :levels] - (face_e + face_w + face_n + face_s) * host)
    base = base + face_n * jnp.concatenate([host[1:], zero], axis=0)
    base = base + face_s * jnp.concatenate([zero, host[:-1]], axis=0)
    for i, part in enumerate((base, face_e, face_w, face_n, face_s)):
        aux[i] = jnp.broadcast_to(part, (COLS, levels))
    copy = pltpu.make_async_copy(aux, aux_out, sems.at[len(sending)])
    copy.start()
    sending.append(copy)
    for copy in sending:
        copy.wait()


def host_kernel(aux, east, west, north, south, out):
    total = aux[0] + (aux[1] * east[...] + aux[2] * west[...])
    rows = row_iota(*total.shape)
    from_north = aux[3] * jnp.broadcast_to(north[0:1], total.shape)
    from_south = aux[4] * jnp.broadcast_to(south[COLS - 1 : COLS], total.shape)
    total = total + jnp.where(rows == COLS - 1, from_north, 0.0)
    out[...] = total + jnp.where(rows == 0, from_south, 0.0)


def neighbours(block):
    found = []
    for axis in ("elem", "band"):
        count = lax.axis_size(axis)
        forward = [(i, (i + 1) % count) for i in range(count)]
        backward = [(target, source) for source, target in forward]
        found.append(lax.ppermute(block, axis, backward))
        found.append(lax.ppermute(block, axis, forward))
    return found


VMEM = pl.BlockSpec(memory_space=pltpu.VMEM)
SMEM = pl.BlockSpec(memory_space=pltpu.SMEM)
HBM = pl.BlockSpec(memory_space=pl.ANY)
STATE = (GROUPS, QUARTER, FIELDS, PAIR, LANES)


def body(
    crm_state, host_state, kappa, substeps, coupling, level_map, field_scale, back_map, back_weight
):
    levels = host_state.shape[0]
    cloud = jnp.transpose(crm_state[0], (1, 0, 2))
    host = jnp.transpose(host_state[:, 0, :], (1, 0))
    own = jnp.concatenate([host, jnp.pad(kappa, ((0, 0), (0, levels - COLS)))], axis=0)
    near = neighbours(own)
    cloud_out, host, aux = pl.pallas_call(
        cloud_kernel,
        out_shape=(
            jax.ShapeDtypeStruct(cloud.shape, BF16),
            jax.ShapeDtypeStruct((COLS, levels), F32),
            jax.ShapeDtypeStruct((5, COLS, levels), F32),
        ),
        in_specs=[HBM] * 12,
        out_specs=(HBM,) * 3,
        scratch_shapes=[pltpu.VMEM(own.shape, F32)] * 5
        + [
            pltpu.VMEM((1, COLS), jnp.int32),
            pltpu.VMEM((NZC, levels), F32),
            pltpu.VMEM((NZC, levels), F32),
            pltpu.SMEM((FIELDS, FIELDS), F32),
            pltpu.SMEM((FIELDS,), F32),
            pltpu.SMEM((FIELDS,), F32),
            pltpu.VMEM(STATE, F32),
            pltpu.VMEM(STATE, F32),
            pltpu.VMEM((GROUPS, QUARTER, PAIR, LANES), F32),
            pltpu.VMEM((GROUPS, FIELDS, PAIR, LANES), F32),
            pltpu.VMEM((LANES, LANES), BF16),
            pltpu.VMEM((FIELDS * PAIR, FIELDS * PAIR), BF16),
            pltpu.VMEM((GROUPS, PAIR, LANES), F32),
            pltpu.VMEM((CELLS, 2 * LANES), BF16),
            pltpu.VMEM((COLS, CELLS), BF16),
            pltpu.SMEM((GROUPS,), jnp.int32),
            pltpu.VMEM((NXC, CELLS), BF16),
            pltpu.VMEM((FIELDS, COLS, CELLS), BF16),
            pltpu.VMEM((FIELDS, COLS, CELLS), BF16),
            pltpu.VMEM((COLS, levels), F32),
            pltpu.VMEM((5, COLS, levels), F32),
            pltpu.SemaphoreType.DMA((FIELDS + 11,)),
        ],
        compiler_params=pltpu.CompilerParams(vmem_limit_bytes=56 * 1024 * 1024),
        name="cloud_windows",
    )(cloud, own, *near, substeps, level_map, back_map.T, coupling, field_scale, back_weight)
    host = pl.pallas_call(
        host_kernel,
        out_shape=jax.ShapeDtypeStruct((COLS, levels), F32),
        in_specs=[VMEM] * 5,
        out_specs=VMEM,
        compiler_params=pltpu.CompilerParams(vmem_limit_bytes=1024 * 1024),
        name="host_section",
    )(aux, *neighbours(host))
    crm_final = jnp.transpose(cloud_out, (1, 0, 2))[None]
    host_final = jnp.transpose(host, (1, 0))[:, None, :]
    return (crm_final, host_final)


def solution(mesh):
    return jax.shard_map(
        body,
        mesh=mesh,
        in_specs=(
            P("elem", "band", None, None),
            P(None, "elem", "band"),
            P("elem", "band"),
            P("elem", "band"),
            P(),
            P(),
            P(),
            P(),
            P(),
        ),
        out_specs=(P("elem", "band", None, None), P(None, "elem", "band")),
        check_vma=False,
    )
```

```python
import jax
import jax.numpy as jnp
from jax import lax
from jax.experimental import pallas as pl
from jax.experimental.pallas import tpu as pltpu
from jax.sharding import PartitionSpec as P

FIELDS = 6
NZC = 60
NXC = 64
SUB = 4
WINDOWS = 2
LANES = 2 * NXC
COLS = 32
SIZE = 8
PAIR = 2 * SIZE
GROUPS = COLS // SIZE
QUARTER = NZC // 4
HALF_TILES = NZC // 4
CELLS = NZC * NXC
CHUNK = 3
CLOUD_STEP = 0.1
F32 = jnp.float32
BF16 = jnp.bfloat16
HIGHEST = lax.Precision.HIGHEST


def row_iota(*shape):
    return lax.broadcasted_iota(jnp.int32, shape, 0)


def lane_iota(*shape):
    return lax.broadcasted_iota(jnp.int32, shape, 1)


def column_of(row):
    square = jnp.broadcast_to(row, (COLS, COLS))
    eye = row_iota(COLS, COLS) == lane_iota(COLS, COLS)
    return jnp.sum(jnp.where(eye, square, 0.0), axis=1, keepdims=True)


def ranks(counts_row):
    rows = row_iota(COLS, COLS)
    lanes = lane_iota(COLS, COLS)
    along_lanes = jnp.broadcast_to(counts_row, (COLS, COLS))
    column = column_of(counts_row)
    along_rows = jnp.broadcast_to(column, (COLS, COLS))
    before = (along_lanes > along_rows) | ((along_lanes == along_rows) & (lanes < rows))
    rank_col = jnp.sum(jnp.where(before, 1.0, 0.0), axis=1, keepdims=True)
    after = (along_rows > along_lanes) | ((along_rows == along_lanes) & (rows < lanes))
    rank_row = jnp.sum(jnp.where(after, 1.0, 0.0), axis=0, keepdims=True)
    to_slot = jnp.where(jnp.broadcast_to(rank_row, (COLS, COLS)) == rows.astype(F32), 1.0, 0.0)
    to_column = jnp.where(jnp.broadcast_to(rank_col, (COLS, COLS)) == lanes.astype(F32), 1.0, 0.0)
    return to_slot, to_column, column


def hi_lo(value):
    hi = value.astype(BF16)
    rest = value - hi.astype(F32)
    mid = rest.astype(BF16)
    return hi, mid, (rest - mid.astype(F32)).astype(BF16)


def permuted(one_hot, value):
    total = None
    for part in hi_lo(value):
        term = jnp.dot(one_hot, part, preferred_element_type=F32)
        total = term if total is None else total + term
    return total


def quarter_of(level):
    part, place = divmod(level, QUARTER)
    half, sub = divmod(part, 2)
    return half, sub, place


def weighted(state, g, zi, weights):
    total = weights[0] * state[g, zi, 0]
    for f in range(1, FIELDS):
        total = total + weights[f] * state[g, zi, f]
    return total


def prepare_force(force, host_sorted, level_map, fscale, expand):
    mapped = lax.dot_general(
        host_sorted, level_map[...], (((1,), (1,)), ((), ())), precision=HIGHEST,
        preferred_element_type=F32,
    )
    mapped = jnp.concatenate([mapped, jnp.zeros((COLS, NXC - NZC), F32)], axis=1)
    hi = mapped.astype(BF16)
    lo = (mapped - hi.astype(F32)).astype(BF16)
    parts = jnp.concatenate([hi, lo], axis=0)
    for zi in range(QUARTER):
        both = jnp.dot(
            parts, expand[:, 2 * zi * LANES : 2 * (zi + 1) * LANES], preferred_element_type=F32
        )
        both = both[:COLS] + both[COLS:]
        for g in range(GROUPS):
            rows = both[g * SIZE : (g + 1) * SIZE]
            spread = jnp.concatenate([rows[:, :LANES], rows[:, LANES:]], axis=0)
            for f in range(FIELDS):
                force[g, zi, f] = fscale[f] * spread


def advance_window(state, force, counts16, most, edge, dmat, cmat):
    low = lane_iota(SIZE, LANES) < NXC

    def substep(turn, active):
        for g in range(active):
            step = jnp.where(counts16[g] > turn.astype(F32), CLOUD_STEP, 0.0)
            keep = 1.0 - 2.0 * step
            prev = []
            for f in range(FIELDS):
                first = state[g, 0, f]
                last = state[g, QUARTER - 1, f]
                edge[g, f] = jnp.concatenate(
                    [first[SIZE:], jnp.where(low, pltpu.roll(first[:SIZE], NXC, 1), 0.0)], axis=0
                )
                prev.append(
                    jnp.concatenate(
                        [jnp.where(low, 0.0, pltpu.roll(last[SIZE:], NXC, 1)), last[:SIZE]], axis=0
                    )
                )
            for start in range(0, QUARTER, CHUNK):
                places = range(start, start + CHUNK)
                flats = [state[g, zi].reshape(FIELDS * PAIR, LANES).astype(BF16) for zi in places]
                slopes = jnp.dot(
                    jnp.concatenate(flats, axis=0), dmat[...], preferred_element_type=F32
                )
                for i, zi in enumerate(places):
                    mixed = jnp.dot(cmat[...], flats[i], preferred_element_type=F32)
                    now = [state[g, zi, f] for f in range(FIELDS)]
                    news = []
                    for f in range(FIELDS):
                        rows = slice(f * PAIR, (f + 1) * PAIR)
                        here = (i * FIELDS + f) * PAIR
                        slope = slopes[here : here + PAIR]
                        after = edge[g, f] if zi == QUARTER - 1 else state[g, zi + 1, f]
                        change = (prev[f] + after) + (
                            now[0] * slope + (jnp.tanh(mixed[rows]) + force[g, zi, f])
                        )
                        news.append(keep * now[f] + step * change)
                    for f in range(FIELDS):
                        state[g, zi, f] = news[f]
                    prev = now

    def body(turn, carry):
        running = sum(jnp.where(most[g] > turn, 1, 0) for g in range(GROUPS))
        for active in range(1, GROUPS + 1):
            pl.when(running == active)(lambda active=active: substep(turn, active))
        return carry

    lax.fori_loop(0, most[0], body, 0)


def differences(state, sums, weights, diffs):
    for zi in range(QUARTER):
        changes = []
        for g in range(GROUPS):
            end = weighted(state, g, zi, weights)
            changes.append(end - sums[g, zi])
            sums[g, zi] = end
        for sub in range(2):
            rows = jnp.concatenate([c[sub * SIZE : (sub + 1) * SIZE] for c in changes], axis=0)
            place = 2 * zi + sub
            diffs[:, place * LANES : (place + 1) * LANES] = rows.astype(BF16)


def tendency(diffs, backx, to_column):
    both = jnp.dot(diffs[...], backx[...], preferred_element_type=F32)
    return permuted(to_column, both[:, :LANES] + both[:, LANES:])


def swapped_halves(low, one, two):
    outer = jnp.where(low, one, two)
    inner = pltpu.roll(jnp.where(low, two, one), NXC, 1)
    return jnp.where(low, outer, inner), jnp.where(low, inner, outer)


def cloud_kernel(
    cloud_in, own_in, band_a_in, elem_a_in, band_b_in, elem_b_in, counts_in, level_in, back_in, coup_in, fscale_in,
    bweight_in,
    cloud_out, host_out, aux_out,
    own, band_a, elem_a, band_b, elem_b, counts, level_map, back_t, coup, fscale, bweight,
    state, force, sums, edge, dmat, cmat, counts16, backx, diffs, most, expand,
    out_buf, cloud, host_buf, aux, sems,
):
    levels = host_out.shape[1]
    sources = (
        own_in, band_a_in, elem_a_in, band_b_in, elem_b_in, counts_in, level_in, back_in, coup_in, fscale_in,
        bweight_in,
    )
    places = (own, band_a, elem_a, band_b, elem_b, counts, level_map, back_t, coup, fscale, bweight)
    copies = [
        pltpu.make_async_copy(src, dst, sems.at[FIELDS + i])
        for i, (src, dst) in enumerate(zip(sources, places))
    ]
    for copy in copies:
        copy.start()
    loads = [
        pltpu.make_async_copy(cloud_in.at[f], cloud.at[f], sems.at[f]) for f in range(FIELDS)
    ]
    for copy in loads:
        copy.start()
    r, l = row_iota(LANES, LANES), lane_iota(LANES, LANES)
    same = (r // NXC) == (l // NXC)
    ahead = same & (r % NXC == (l + 1) % NXC)
    behind = same & (r % NXC == (l + NXC - 1) % NXC)
    dmat[...] = (jnp.where(behind, 0.5, 0.0) - jnp.where(ahead, 0.5, 0.0)).astype(BF16)
    r, l = row_iota(NXC, LANES), lane_iota(NXC, LANES)
    for zi in range(QUARTER):
        for sub in range(2):
            level = sub * QUARTER + zi
            level = jnp.where(l < NXC, level, level + 2 * QUARTER)
            part = slice((2 * zi + sub) * LANES, (2 * zi + sub + 1) * LANES)
            expand[:, part] = jnp.where(r == level, 1.0, 0.0).astype(BF16)
    for copy in copies:
        copy.wait()

    counts_row = counts[...].astype(F32)
    to_slot, to_column, column = ranks(counts_row)
    to_slot = to_slot.astype(BF16)
    to_column = to_column.astype(BF16)
    over = [jnp.sum(jnp.where(counts[...] > turn, 1, 0)) for turn in range(1, SUB)]
    for g in range(GROUPS):
        most[g] = 1 + sum(jnp.where(over_turn > g * SIZE, 1, 0) for over_turn in over)
    counts_sorted = jnp.dot(
        to_slot, jnp.broadcast_to(column, (COLS, LANES)).astype(BF16), preferred_element_type=F32
    )
    for g in range(GROUPS):
        rows = counts_sorted[g * SIZE : (g + 1) * SIZE]
        counts16[g] = jnp.concatenate([rows, rows], axis=0)
    weights = [bweight[f] for f in range(FIELDS)]

    r, l = row_iota(FIELDS * PAIR, FIELDS * PAIR), lane_iota(FIELDS * PAIR, FIELDS * PAIR)
    same = (r % PAIR) == (l % PAIR)
    mixer = jnp.zeros((FIELDS * PAIR, FIELDS * PAIR), F32)
    for f in range(FIELDS):
        for other in range(FIELDS):
            here = same & (r // PAIR == f) & (l // PAIR == other)
            mixer = jnp.where(here, coup[f, other], mixer)
    cmat[...] = mixer.astype(BF16)
    padding = jnp.zeros((1, LANES - levels), F32)
    for zi in range(QUARTER):
        for sub in range(2):
            for half in range(2):
                level = (2 * half + sub) * QUARTER + zi
                row = jnp.concatenate([back_t[level : level + 1, :], padding], axis=1) * (1.0 / NXC)
                hi = row.astype(BF16)
                lo = (row - hi.astype(F32)).astype(BF16)
                first = ((2 * zi + sub) * 2 + half) * NXC
                backx[first : first + NXC, :LANES] = jnp.broadcast_to(hi, (NXC, LANES))
                backx[first : first + NXC, LANES:] = jnp.broadcast_to(lo, (NXC, LANES))

    even = lax.rem(lax.axis_index("band"), 2) == 0
    north = jnp.where(even, band_a[...], band_b[...])
    south = jnp.where(even, band_b[...], band_a[...])
    host = own[:COLS]
    kap, kap_a, kap_b, kap_n, kap_s = (
        column_of(ref[COLS : COLS + 1, :COLS]) for ref in (own, elem_a, elem_b, north, south)
    )
    face_a = 0.5 * (kap + kap_a)
    face_b = 0.5 * (kap + kap_b)
    face_n = 0.5 * (kap + jnp.concatenate([kap[1:], kap_n[:1]], axis=0))
    face_s = 0.5 * (kap + jnp.concatenate([kap_s[COLS - 1 :], kap[:-1]], axis=0))
    spread = face_a * (elem_a[:COLS] - host) + face_b * (elem_b[:COLS] - host)
    spread = spread + face_n * (jnp.concatenate([host[1:], north[0:1]], axis=0) - host)
    spread = spread + face_s * (
        jnp.concatenate([south[COLS - 1 : COLS], host[:-1]], axis=0) - host
    )

    prepare_force(force, permuted(to_slot, host), level_map, fscale, expand)

    low = lane_iota(COLS, LANES) < NXC
    for copy in loads:
        copy.wait()
    for f in range(FIELDS):
        for tile in range(HALF_TILES):
            near = slice(tile * LANES, (tile + 1) * LANES)
            far = slice((tile + HALF_TILES) * LANES, (tile + HALF_TILES + 1) * LANES)
            _, sub, place = quarter_of(2 * tile)
            _, sub2, place2 = quarter_of(2 * tile + 1)
            both = jnp.concatenate(swapped_halves(low, cloud[f, :, near], cloud[f, :, far]), axis=1)
            both = jnp.dot(to_slot, both, preferred_element_type=F32)
            for g in range(GROUPS):
                rows = both[g * SIZE : (g + 1) * SIZE]
                state[g, place, f, sub * SIZE : (sub + 1) * SIZE, :] = rows[:, :LANES]
                state[g, place2, f, sub2 * SIZE : (sub2 + 1) * SIZE, :] = rows[:, LANES:]
    for g in range(GROUPS):
        for zi in range(QUARTER):
            sums[g, zi] = weighted(state, g, zi, weights)

    advance_window(state, force, counts16, most, edge, dmat, cmat)
    differences(state, sums, weights, diffs)
    tend = tendency(diffs, backx, to_column)
    host = host + (tend[:, :levels] + spread)
    host_buf[...] = host
    sending = [pltpu.make_async_copy(host_buf, host_out, sems.at[0])]
    sending[0].start()
    prepare_force(force, permuted(to_slot, host), level_map, fscale, expand)
    advance_window(state, force, counts16, most, edge, dmat, cmat)
    for fields in (range(0, FIELDS // 2), range(FIELDS // 2, FIELDS)):
        for tile in range(HALF_TILES):
            near = slice(tile * LANES, (tile + 1) * LANES)
            far = slice((tile + HALF_TILES) * LANES, (tile + HALF_TILES + 1) * LANES)
            _, sub, place = quarter_of(2 * tile)
            _, sub2, place2 = quarter_of(2 * tile + 1)
            for f in fields:
                rows = jnp.concatenate(
                    [
                        jnp.concatenate(
                            [
                                state[g, place, f, sub * SIZE : (sub + 1) * SIZE, :],
                                state[g, place2, f, sub2 * SIZE : (sub2 + 1) * SIZE, :],
                            ],
                            axis=1,
                        )
                        for g in range(GROUPS)
                    ],
                    axis=0,
                )
                out = jnp.dot(to_column, rows.astype(BF16), preferred_element_type=F32).astype(BF16)
                one, two = swapped_halves(low, out[:, :LANES], out[:, LANES:])
                out_buf[f, :, near] = one
                out_buf[f, :, far] = two
        for f in fields:
            copy = pltpu.make_async_copy(out_buf.at[f], cloud_out.at[f], sems.at[len(sending)])
            copy.start()
            sending.append(copy)
    differences(state, sums, weights, diffs)

    tend = tendency(diffs, backx, to_column)
    zero = jnp.zeros((1, levels), F32)
    base = host + (tend[:, :levels] - (face_a + face_b + face_n + face_s) * host)
    base = base + face_n * jnp.concatenate([host[1:], zero], axis=0)
    base = base + face_s * jnp.concatenate([zero, host[:-1]], axis=0)
    room = jnp.zeros((COLS, LANES - levels - 4), F32)
    aux[...] = jnp.concatenate([base, face_a, face_b, face_n, face_s, room], axis=1)
    copy = pltpu.make_async_copy(aux, aux_out, sems.at[len(sending)])
    copy.start()
    sending.append(copy)
    for copy in sending:
        copy.wait()


def host_kernel(aux, band_a, elem_a, band_b, elem_b, out):
    levels = out.shape[1]
    face_a, face_b, face_n, face_s = (aux[:, levels + i : levels + i + 1] for i in range(4))
    total = aux[:, :levels] + (face_a * elem_a[...] + face_b * elem_b[...])
    even = lax.rem(lax.axis_index("band"), 2) == 0
    north = jnp.where(even, band_a[0:1], band_b[0:1])
    south = jnp.where(even, band_b[COLS - 1 : COLS], band_a[COLS - 1 : COLS])
    rows = row_iota(*total.shape)
    total = total + jnp.where(rows == COLS - 1, face_n * north, 0.0)
    out[...] = total + jnp.where(rows == 0, face_s * south, 0.0)


def neighbours(block):
    found = []
    for odd in range(2):
        for axis in ("band", "elem"):
            count = lax.axis_size(axis)
            pairs = [(i, (i + 1 - 2 * ((i + odd) % 2)) % count) for i in range(count)]
            found.append(lax.ppermute(block, axis, pairs))
    return found


VMEM = pl.BlockSpec(memory_space=pltpu.VMEM)
SMEM = pl.BlockSpec(memory_space=pltpu.SMEM)
HBM = pl.BlockSpec(memory_space=pl.ANY)
STATE = (GROUPS, QUARTER, FIELDS, PAIR, LANES)


def body(
    crm_state, host_state, kappa, substeps, coupling, level_map, field_scale, back_map, back_weight
):
    levels = host_state.shape[0]
    cloud = jnp.transpose(crm_state[0], (1, 0, 2))
    host = jnp.transpose(host_state[:, 0, :], (1, 0))
    own = jnp.concatenate([host, jnp.pad(kappa, ((0, 0), (0, levels - COLS)))], axis=0)
    near = neighbours(own)
    cloud_out, host, aux = pl.pallas_call(
        cloud_kernel,
        out_shape=(
            jax.ShapeDtypeStruct(cloud.shape, BF16),
            jax.ShapeDtypeStruct((COLS, levels), F32),
            jax.ShapeDtypeStruct((COLS, LANES), F32),
        ),
        in_specs=[HBM] * 12,
        out_specs=(HBM,) * 3,
        scratch_shapes=[pltpu.VMEM(own.shape, F32)] * 5
        + [
            pltpu.VMEM((1, COLS), jnp.int32),
            pltpu.VMEM((NZC, levels), F32),
            pltpu.VMEM((NZC, levels), F32),
            pltpu.SMEM((FIELDS, FIELDS), F32),
            pltpu.SMEM((FIELDS,), F32),
            pltpu.SMEM((FIELDS,), F32),
            pltpu.VMEM(STATE, F32),
            pltpu.VMEM(STATE, F32),
            pltpu.VMEM((GROUPS, QUARTER, PAIR, LANES), F32),
            pltpu.VMEM((GROUPS, FIELDS, PAIR, LANES), F32),
            pltpu.VMEM((LANES, LANES), BF16),
            pltpu.VMEM((FIELDS * PAIR, FIELDS * PAIR), BF16),
            pltpu.VMEM((GROUPS, PAIR, LANES), F32),
            pltpu.VMEM((CELLS, 2 * LANES), BF16),
            pltpu.VMEM((COLS, CELLS), BF16),
            pltpu.SMEM((GROUPS,), jnp.int32),
            pltpu.VMEM((NXC, CELLS), BF16),
            pltpu.VMEM((FIELDS, COLS, CELLS), BF16),
            pltpu.VMEM((FIELDS, COLS, CELLS), BF16),
            pltpu.VMEM((COLS, levels), F32),
            pltpu.VMEM((COLS, LANES), F32),
            pltpu.SemaphoreType.DMA((FIELDS + 11,)),
        ],
        compiler_params=pltpu.CompilerParams(vmem_limit_bytes=56 * 1024 * 1024),
        name="cloud_windows",
    )(cloud, own, *near, substeps, level_map, back_map.T, coupling, field_scale, back_weight)
    host = pl.pallas_call(
        host_kernel,
        out_shape=jax.ShapeDtypeStruct((COLS, levels), F32),
        in_specs=[VMEM] * 5,
        out_specs=VMEM,
        compiler_params=pltpu.CompilerParams(vmem_limit_bytes=1024 * 1024),
        name="host_section",
    )(aux, *neighbours(host))
    crm_final = jnp.transpose(cloud_out, (1, 0, 2))[None]
    host_final = jnp.transpose(host, (1, 0))[:, None, :]
    return (crm_final, host_final)


def solution(mesh):
    return jax.shard_map(
        body,
        mesh=mesh,
        in_specs=(
            P("elem", "band", None, None),
            P(None, "elem", "band"),
            P("elem", "band"),
            P("elem", "band"),
            P(),
            P(),
            P(),
            P(),
            P(),
        ),
        out_specs=(P("elem", "band", None, None), P(None, "elem", "band")),
        check_vma=False,
    )
```

```python
import jax
import jax.numpy as jnp
from jax import lax
from jax.experimental import pallas as pl
from jax.experimental.pallas import tpu as pltpu
from jax.sharding import PartitionSpec as P

FIELDS = 6
NZC = 60
NXC = 64
SUB = 4
WINDOWS = 2
LANES = 2 * NXC
COLS = 32
SIZE = 8
PAIR = 2 * SIZE
GROUPS = COLS // SIZE
QUARTER = NZC // 4
HALF_TILES = NZC // 4
CELLS = NZC * NXC
CHUNK = 5
CLOUD_STEP = 0.1
F32 = jnp.float32
BF16 = jnp.bfloat16
HIGHEST = lax.Precision.HIGHEST


def row_iota(*shape):
    return lax.broadcasted_iota(jnp.int32, shape, 0)


def lane_iota(*shape):
    return lax.broadcasted_iota(jnp.int32, shape, 1)


def column_of(row):
    square = jnp.broadcast_to(row, (COLS, COLS))
    eye = row_iota(COLS, COLS) == lane_iota(COLS, COLS)
    return jnp.sum(jnp.where(eye, square, 0.0), axis=1, keepdims=True)


def ranks(counts_row):
    rows = row_iota(COLS, COLS)
    lanes = lane_iota(COLS, COLS)
    along_lanes = jnp.broadcast_to(counts_row, (COLS, COLS))
    column = column_of(counts_row)
    along_rows = jnp.broadcast_to(column, (COLS, COLS))
    before = (along_lanes > along_rows) | ((along_lanes == along_rows) & (lanes < rows))
    rank_col = jnp.sum(jnp.where(before, 1.0, 0.0), axis=1, keepdims=True)
    after = (along_rows > along_lanes) | ((along_rows == along_lanes) & (rows < lanes))
    rank_row = jnp.sum(jnp.where(after, 1.0, 0.0), axis=0, keepdims=True)
    to_slot = jnp.where(jnp.broadcast_to(rank_row, (COLS, COLS)) == rows.astype(F32), 1.0, 0.0)
    to_column = jnp.where(jnp.broadcast_to(rank_col, (COLS, COLS)) == lanes.astype(F32), 1.0, 0.0)
    return to_slot, to_column, column


def hi_lo(value):
    hi = value.astype(BF16)
    rest = value - hi.astype(F32)
    mid = rest.astype(BF16)
    return hi, mid, (rest - mid.astype(F32)).astype(BF16)


def permuted(one_hot, value):
    total = None
    for part in hi_lo(value):
        term = jnp.dot(one_hot, part, preferred_element_type=F32)
        total = term if total is None else total + term
    return total


def quarter_of(level):
    part, place = divmod(level, QUARTER)
    half, sub = divmod(part, 2)
    return half, sub, place


def weighted(state, g, zi, weights):
    total = weights[0] * state[g, zi, 0]
    for f in range(1, FIELDS):
        total = total + weights[f] * state[g, zi, f]
    return total


def prepare_force(force, host_sorted, level_map, fscale, expand):
    mapped = lax.dot_general(
        host_sorted, level_map[...], (((1,), (1,)), ((), ())), precision=HIGHEST,
        preferred_element_type=F32,
    )
    mapped = jnp.concatenate([mapped, jnp.zeros((COLS, NXC - NZC), F32)], axis=1)
    hi = mapped.astype(BF16)
    lo = (mapped - hi.astype(F32)).astype(BF16)
    parts = jnp.concatenate([hi, lo], axis=0)
    for zi in range(QUARTER):
        both = jnp.dot(
            parts, expand[:, 2 * zi * LANES : 2 * (zi + 1) * LANES], preferred_element_type=F32
        )
        both = both[:COLS] + both[COLS:]
        for g in range(GROUPS):
            rows = both[g * SIZE : (g + 1) * SIZE]
            spread = jnp.concatenate([rows[:, :LANES], rows[:, LANES:]], axis=0)
            for f in range(FIELDS):
                force[g, zi, f] = fscale[f] * spread


def advance_window(state, force, counts16, most, edge, dmat, cmat):
    low = lane_iota(SIZE, LANES) < NXC

    def substep(turn, active):
        for g in range(active):
            step = jnp.where(counts16[g] > turn.astype(F32), CLOUD_STEP, 0.0)
            keep = 1.0 - 2.0 * step
            prev = []
            for f in range(FIELDS):
                first = state[g, 0, f]
                last = state[g, QUARTER - 1, f]
                edge[g, f] = jnp.concatenate(
                    [first[SIZE:], jnp.where(low, pltpu.roll(first[:SIZE], NXC, 1), 0.0)], axis=0
                )
                prev.append(
                    jnp.concatenate(
                        [jnp.where(low, 0.0, pltpu.roll(last[SIZE:], NXC, 1)), last[:SIZE]], axis=0
                    )
                )
            for start in range(0, QUARTER, CHUNK):
                places = range(start, start + CHUNK)
                flats = [state[g, zi].reshape(FIELDS * PAIR, LANES).astype(BF16) for zi in places]
                slopes = jnp.dot(
                    jnp.concatenate(flats, axis=0), dmat[...], preferred_element_type=F32
                )
                for i, zi in enumerate(places):
                    mixed = jnp.dot(cmat[...], flats[i], preferred_element_type=F32)
                    now = [state[g, zi, f] for f in range(FIELDS)]
                    news = []
                    for f in range(FIELDS):
                        rows = slice(f * PAIR, (f + 1) * PAIR)
                        here = (i * FIELDS + f) * PAIR
                        slope = slopes[here : here + PAIR]
                        after = edge[g, f] if zi == QUARTER - 1 else state[g, zi + 1, f]
                        change = (prev[f] + after) + (
                            now[0] * slope + (jnp.tanh(mixed[rows]) + force[g, zi, f])
                        )
                        news.append(keep * now[f] + step * change)
                    for f in range(FIELDS):
                        state[g, zi, f] = news[f]
                    prev = now

    def body(turn, carry):
        running = sum(jnp.where(most[g] > turn, 1, 0) for g in range(GROUPS))
        for active in range(1, GROUPS + 1):
            pl.when(running == active)(lambda active=active: substep(turn, active))
        return carry

    lax.fori_loop(0, most[0], body, 0)


def differences(state, sums, weights, diffs):
    for zi in range(QUARTER):
        changes = []
        for g in range(GROUPS):
            end = weighted(state, g, zi, weights)
            changes.append(end - sums[g, zi])
            sums[g, zi] = end
        for sub in range(2):
            rows = jnp.concatenate([c[sub * SIZE : (sub + 1) * SIZE] for c in changes], axis=0)
            place = 2 * zi + sub
            diffs[:, place * LANES : (place + 1) * LANES] = rows.astype(BF16)


def tendency(diffs, backx):
    both = jnp.dot(diffs[...], backx[...], preferred_element_type=F32)
    return both[:, :LANES] + both[:, LANES:]


def swapped_halves(low, one, two):
    outer = jnp.where(low, one, two)
    inner = pltpu.roll(jnp.where(low, two, one), NXC, 1)
    return jnp.where(low, outer, inner), jnp.where(low, inner, outer)


def cloud_kernel(
    cloud_in, own_in, band_a_in, elem_b_in, elem_a_in, band_b_in, counts_in, level_in, back_in, coup_in, fscale_in,
    bweight_in,
    cloud_out, host_out, aux_out,
    own, band_a, elem_b, elem_a, band_b, counts, level_map, back_t, coup, fscale, bweight,
    state, force, sums, edge, dmat, cmat, counts16, backx, diffs, most, expand,
    out_buf, cloud, host_buf, aux, sems,
):
    levels = host_out.shape[1]
    sources = (
        own_in, band_a_in, elem_b_in, elem_a_in, band_b_in, counts_in, level_in, back_in, coup_in, fscale_in,
        bweight_in,
    )
    places = (own, band_a, elem_b, elem_a, band_b, counts, level_map, back_t, coup, fscale, bweight)
    copies = [
        pltpu.make_async_copy(src, dst, sems.at[FIELDS + i])
        for i, (src, dst) in enumerate(zip(sources, places))
    ]
    for copy in copies:
        copy.start()
    loads = [
        pltpu.make_async_copy(cloud_in.at[f], cloud.at[f], sems.at[f]) for f in range(FIELDS)
    ]
    for copy in loads:
        copy.start()
    r, l = row_iota(LANES, LANES), lane_iota(LANES, LANES)
    same = (r // NXC) == (l // NXC)
    ahead = same & (r % NXC == (l + 1) % NXC)
    behind = same & (r % NXC == (l + NXC - 1) % NXC)
    dmat[...] = (jnp.where(behind, 0.5, 0.0) - jnp.where(ahead, 0.5, 0.0)).astype(BF16)
    r, l = row_iota(NXC, LANES), lane_iota(NXC, LANES)
    for zi in range(QUARTER):
        for sub in range(2):
            level = sub * QUARTER + zi
            level = jnp.where(l < NXC, level, level + 2 * QUARTER)
            part = slice((2 * zi + sub) * LANES, (2 * zi + sub + 1) * LANES)
            expand[:, part] = jnp.where(r == level, 1.0, 0.0).astype(BF16)
    for copy in copies:
        copy.wait()

    counts_row = counts[...].astype(F32)
    to_slot, to_column, column = ranks(counts_row)
    to_slot = to_slot.astype(BF16)
    to_column = to_column.astype(BF16)
    over = [jnp.sum(jnp.where(counts[...] > turn, 1, 0)) for turn in range(1, SUB)]
    for g in range(GROUPS):
        most[g] = 1 + sum(jnp.where(over_turn > g * SIZE, 1, 0) for over_turn in over)
    counts_sorted = jnp.dot(
        to_slot, jnp.broadcast_to(column, (COLS, LANES)).astype(BF16), preferred_element_type=F32
    )
    for g in range(GROUPS):
        rows = counts_sorted[g * SIZE : (g + 1) * SIZE]
        counts16[g] = jnp.concatenate([rows, rows], axis=0)
    weights = [bweight[f] for f in range(FIELDS)]

    r, l = row_iota(FIELDS * PAIR, FIELDS * PAIR), lane_iota(FIELDS * PAIR, FIELDS * PAIR)
    same = (r % PAIR) == (l % PAIR)
    mixer = jnp.zeros((FIELDS * PAIR, FIELDS * PAIR), F32)
    for f in range(FIELDS):
        for other in range(FIELDS):
            here = same & (r // PAIR == f) & (l // PAIR == other)
            mixer = jnp.where(here, coup[f, other], mixer)
    cmat[...] = mixer.astype(BF16)
    padding = jnp.zeros((1, LANES - levels), F32)
    for zi in range(QUARTER):
        for sub in range(2):
            for half in range(2):
                level = (2 * half + sub) * QUARTER + zi
                row = jnp.concatenate([back_t[level : level + 1, :], padding], axis=1) * (1.0 / NXC)
                hi = row.astype(BF16)
                lo = (row - hi.astype(F32)).astype(BF16)
                first = ((2 * zi + sub) * 2 + half) * NXC
                backx[first : first + NXC, :LANES] = jnp.broadcast_to(hi, (NXC, LANES))
                backx[first : first + NXC, LANES:] = jnp.broadcast_to(lo, (NXC, LANES))

    even = lax.rem(lax.axis_index("band"), 2) == 0
    north = jnp.where(even, band_a[...], band_b[...])
    south = jnp.where(even, band_b[...], band_a[...])
    host = own[:COLS]
    kap, kap_a, kap_b, kap_n, kap_s = (
        column_of(ref[COLS : COLS + 1, :COLS]) for ref in (own, elem_a, elem_b, north, south)
    )
    face_a = 0.5 * (kap + kap_a)
    face_b = 0.5 * (kap + kap_b)
    face_n = 0.5 * (kap + jnp.concatenate([kap[1:], kap_n[:1]], axis=0))
    face_s = 0.5 * (kap + jnp.concatenate([kap_s[COLS - 1 :], kap[:-1]], axis=0))
    spread = face_a * (elem_a[:COLS] - host) + face_b * (elem_b[:COLS] - host)
    spread = spread + face_n * (jnp.concatenate([host[1:], north[0:1]], axis=0) - host)
    spread = spread + face_s * (
        jnp.concatenate([south[COLS - 1 : COLS], host[:-1]], axis=0) - host
    )

    host_sorted = permuted(to_slot, host)
    prepare_force(force, host_sorted, level_map, fscale, expand)
    spread_sorted = permuted(to_slot, spread)

    low = lane_iota(COLS, LANES) < NXC
    for copy in loads:
        copy.wait()
    for f in range(FIELDS):
        for tile in range(HALF_TILES):
            near = slice(tile * LANES, (tile + 1) * LANES)
            far = slice((tile + HALF_TILES) * LANES, (tile + HALF_TILES + 1) * LANES)
            _, sub, place = quarter_of(2 * tile)
            _, sub2, place2 = quarter_of(2 * tile + 1)
            both = jnp.concatenate(swapped_halves(low, cloud[f, :, near], cloud[f, :, far]), axis=1)
            both = jnp.dot(to_slot, both, preferred_element_type=F32)
            for g in range(GROUPS):
                rows = both[g * SIZE : (g + 1) * SIZE]
                state[g, place, f, sub * SIZE : (sub + 1) * SIZE, :] = rows[:, :LANES]
                state[g, place2, f, sub2 * SIZE : (sub2 + 1) * SIZE, :] = rows[:, LANES:]
    for g in range(GROUPS):
        for zi in range(QUARTER):
            sums[g, zi] = weighted(state, g, zi, weights)

    advance_window(state, force, counts16, most, edge, dmat, cmat)
    differences(state, sums, weights, diffs)
    tend_sorted = tendency(diffs, backx)
    host_sorted = host_sorted + (tend_sorted[:, :levels] + spread_sorted)
    prepare_force(force, host_sorted, level_map, fscale, expand)
    tend = permuted(to_column, tend_sorted)
    host = host + (tend[:, :levels] + spread)
    host_buf[...] = host
    sending = [pltpu.make_async_copy(host_buf, host_out, sems.at[0])]
    sending[0].start()
    advance_window(state, force, counts16, most, edge, dmat, cmat)
    for fields in (range(0, FIELDS // 2), range(FIELDS // 2, FIELDS)):
        for tile in range(HALF_TILES):
            near = slice(tile * LANES, (tile + 1) * LANES)
            far = slice((tile + HALF_TILES) * LANES, (tile + HALF_TILES + 1) * LANES)
            _, sub, place = quarter_of(2 * tile)
            _, sub2, place2 = quarter_of(2 * tile + 1)
            for f in fields:
                rows = jnp.concatenate(
                    [
                        jnp.concatenate(
                            [
                                state[g, place, f, sub * SIZE : (sub + 1) * SIZE, :],
                                state[g, place2, f, sub2 * SIZE : (sub2 + 1) * SIZE, :],
                            ],
                            axis=1,
                        )
                        for g in range(GROUPS)
                    ],
                    axis=0,
                )
                out = jnp.dot(to_column, rows.astype(BF16), preferred_element_type=F32).astype(BF16)
                one, two = swapped_halves(low, out[:, :LANES], out[:, LANES:])
                out_buf[f, :, near] = one
                out_buf[f, :, far] = two
        for f in fields:
            copy = pltpu.make_async_copy(out_buf.at[f], cloud_out.at[f], sems.at[len(sending)])
            copy.start()
            sending.append(copy)
    differences(state, sums, weights, diffs)

    tend = permuted(to_column, tendency(diffs, backx))
    zero = jnp.zeros((1, levels), F32)
    base = host + (tend[:, :levels] - (face_a + face_b + face_n + face_s) * host)
    base = base + face_n * jnp.concatenate([host[1:], zero], axis=0)
    base = base + face_s * jnp.concatenate([zero, host[:-1]], axis=0)
    room = jnp.zeros((COLS, LANES - levels - 4), F32)
    aux[...] = jnp.concatenate([base, face_a, face_b, face_n, face_s, room], axis=1)
    copy = pltpu.make_async_copy(aux, aux_out, sems.at[len(sending)])
    copy.start()
    sending.append(copy)
    for copy in sending:
        copy.wait()


def host_kernel(aux, band_a, elem_a, band_b, elem_b, out):
    levels = out.shape[1]
    face_a, face_b, face_n, face_s = (aux[:, levels + i : levels + i + 1] for i in range(4))
    total = aux[:, :levels] + (face_a * elem_a[...] + face_b * elem_b[...])
    even = lax.rem(lax.axis_index("band"), 2) == 0
    north = jnp.where(even, band_a[0:1], band_b[0:1])
    south = jnp.where(even, band_b[COLS - 1 : COLS], band_a[COLS - 1 : COLS])
    rows = row_iota(*total.shape)
    total = total + jnp.where(rows == COLS - 1, face_n * north, 0.0)
    out[...] = total + jnp.where(rows == 0, face_s * south, 0.0)


def neighbours(block):
    found = []
    for odd in range(2):
        for axis in ("band", "elem"):
            count = lax.axis_size(axis)
            pairs = [(i, (i + 1 - 2 * ((i + odd) % 2)) % count) for i in range(count)]
            found.append(lax.ppermute(block, axis, pairs))
    return found


VMEM = pl.BlockSpec(memory_space=pltpu.VMEM)
SMEM = pl.BlockSpec(memory_space=pltpu.SMEM)
HBM = pl.BlockSpec(memory_space=pl.ANY)
STATE = (GROUPS, QUARTER, FIELDS, PAIR, LANES)


def body(
    crm_state, host_state, kappa, substeps, coupling, level_map, field_scale, back_map, back_weight
):
    levels = host_state.shape[0]
    cloud = jnp.transpose(crm_state[0], (1, 0, 2))
    host = jnp.transpose(host_state[:, 0, :], (1, 0))
    own = jnp.concatenate([host, jnp.pad(kappa, ((0, 0), (0, levels - COLS)))], axis=0)
    band_a, elem_a, band_b, elem_b = neighbours(own)
    near = (band_a, elem_b, elem_a, band_b)
    cloud_out, host, aux = pl.pallas_call(
        cloud_kernel,
        out_shape=(
            jax.ShapeDtypeStruct(cloud.shape, BF16),
            jax.ShapeDtypeStruct((COLS, levels), F32),
            jax.ShapeDtypeStruct((COLS, LANES), F32),
        ),
        in_specs=[HBM] * 12,
        out_specs=(HBM,) * 3,
        scratch_shapes=[pltpu.VMEM(own.shape, F32)] * 5
        + [
            pltpu.VMEM((1, COLS), jnp.int32),
            pltpu.VMEM((NZC, levels), F32),
            pltpu.VMEM((NZC, levels), F32),
            pltpu.SMEM((FIELDS, FIELDS), F32),
            pltpu.SMEM((FIELDS,), F32),
            pltpu.SMEM((FIELDS,), F32),
            pltpu.VMEM(STATE, F32),
            pltpu.VMEM(STATE, F32),
            pltpu.VMEM((GROUPS, QUARTER, PAIR, LANES), F32),
            pltpu.VMEM((GROUPS, FIELDS, PAIR, LANES), F32),
            pltpu.VMEM((LANES, LANES), BF16),
            pltpu.VMEM((FIELDS * PAIR, FIELDS * PAIR), BF16),
            pltpu.VMEM((GROUPS, PAIR, LANES), F32),
            pltpu.VMEM((CELLS, 2 * LANES), BF16),
            pltpu.VMEM((COLS, CELLS), BF16),
            pltpu.SMEM((GROUPS,), jnp.int32),
            pltpu.VMEM((NXC, CELLS), BF16),
            pltpu.VMEM((FIELDS, COLS, CELLS), BF16),
            pltpu.VMEM((FIELDS, COLS, CELLS), BF16),
            pltpu.VMEM((COLS, levels), F32),
            pltpu.VMEM((COLS, LANES), F32),
            pltpu.SemaphoreType.DMA((FIELDS + 11,)),
        ],
        compiler_params=pltpu.CompilerParams(vmem_limit_bytes=56 * 1024 * 1024),
        name="cloud_windows",
    )(cloud, own, *near, substeps, level_map, back_map.T, coupling, field_scale, back_weight)
    host = pl.pallas_call(
        host_kernel,
        out_shape=jax.ShapeDtypeStruct((COLS, levels), F32),
        in_specs=[VMEM] * 5,
        out_specs=VMEM,
        compiler_params=pltpu.CompilerParams(vmem_limit_bytes=1024 * 1024),
        name="host_section",
    )(aux, *neighbours(host))
    crm_final = jnp.transpose(cloud_out, (1, 0, 2))[None]
    host_final = jnp.transpose(host, (1, 0))[:, None, :]
    return (crm_final, host_final)


def solution(mesh):
    return jax.shard_map(
        body,
        mesh=mesh,
        in_specs=(
            P("elem", "band", None, None),
            P(None, "elem", "band"),
            P("elem", "band"),
            P("elem", "band"),
            P(),
            P(),
            P(),
            P(),
            P(),
        ),
        out_specs=(P("elem", "band", None, None), P(None, "elem", "band")),
        check_vma=False,
    )
```

```python
import jax
import jax.numpy as jnp
from jax import lax
from jax.experimental import pallas as pl
from jax.experimental.pallas import tpu as pltpu
from jax.sharding import PartitionSpec as P

FIELDS = 6
NZC = 60
NXC = 64
SUB = 4
WINDOWS = 2
LANES = 2 * NXC
COLS = 32
SIZE = 8
PAIR = 2 * SIZE
GROUPS = COLS // SIZE
QUARTER = NZC // 4
HALF_TILES = NZC // 4
CELLS = NZC * NXC
CHUNK = 5
CLOUD_STEP = 0.1
F32 = jnp.float32
BF16 = jnp.bfloat16
HIGHEST = lax.Precision.HIGHEST


def row_iota(*shape):
    return lax.broadcasted_iota(jnp.int32, shape, 0)


def lane_iota(*shape):
    return lax.broadcasted_iota(jnp.int32, shape, 1)


def column_of(row):
    square = jnp.broadcast_to(row, (COLS, COLS))
    eye = row_iota(COLS, COLS) == lane_iota(COLS, COLS)
    return jnp.sum(jnp.where(eye, square, 0.0), axis=1, keepdims=True)


def ranks(counts_row):
    rows = row_iota(COLS, COLS)
    lanes = lane_iota(COLS, COLS)
    along_lanes = jnp.broadcast_to(counts_row, (COLS, COLS))
    column = column_of(counts_row)
    along_rows = jnp.broadcast_to(column, (COLS, COLS))
    before = (along_lanes > along_rows) | ((along_lanes == along_rows) & (lanes < rows))
    rank_col = jnp.sum(jnp.where(before, 1.0, 0.0), axis=1, keepdims=True)
    after = (along_rows > along_lanes) | ((along_rows == along_lanes) & (rows < lanes))
    rank_row = jnp.sum(jnp.where(after, 1.0, 0.0), axis=0, keepdims=True)
    to_slot = jnp.where(jnp.broadcast_to(rank_row, (COLS, COLS)) == rows.astype(F32), 1.0, 0.0)
    to_column = jnp.where(jnp.broadcast_to(rank_col, (COLS, COLS)) == lanes.astype(F32), 1.0, 0.0)
    return to_slot, to_column, column


def hi_lo(value):
    hi = value.astype(BF16)
    rest = value - hi.astype(F32)
    mid = rest.astype(BF16)
    return hi, mid, (rest - mid.astype(F32)).astype(BF16)


def permuted(one_hot, value):
    total = None
    for part in hi_lo(value):
        term = jnp.dot(one_hot, part, preferred_element_type=F32)
        total = term if total is None else total + term
    return total


def quarter_of(level):
    part, place = divmod(level, QUARTER)
    half, sub = divmod(part, 2)
    return half, sub, place


def weighted(state, g, zi, weights):
    total = weights[0] * state[g, zi, 0]
    for f in range(1, FIELDS):
        total = total + weights[f] * state[g, zi, f]
    return total


def prepare_force(force, host_sorted, level_map, fscale, expand):
    mapped = lax.dot_general(
        host_sorted, level_map[...], (((1,), (1,)), ((), ())), precision=HIGHEST,
        preferred_element_type=F32,
    )
    mapped = jnp.concatenate([mapped, jnp.zeros((COLS, NXC - NZC), F32)], axis=1)
    hi = mapped.astype(BF16)
    lo = (mapped - hi.astype(F32)).astype(BF16)
    parts = jnp.concatenate([hi, lo], axis=0)
    for zi in range(QUARTER):
        both = jnp.dot(
            parts, expand[:, 2 * zi * LANES : 2 * (zi + 1) * LANES], preferred_element_type=F32
        )
        both = both[:COLS] + both[COLS:]
        for g in range(GROUPS):
            rows = both[g * SIZE : (g + 1) * SIZE]
            spread = jnp.concatenate([rows[:, :LANES], rows[:, LANES:]], axis=0)
            for f in range(FIELDS):
                force[g, zi, f] = fscale[f] * spread


def advance_window(state, force, counts16, most, edge, dmat, cmat):
    low = lane_iota(SIZE, LANES) < NXC

    def substep(turn, active):
        for g in range(active):
            step = jnp.where(counts16[g] > turn.astype(F32), CLOUD_STEP, 0.0)
            keep = 1.0 - 2.0 * step
            prev = []
            for f in range(FIELDS):
                first = state[g, 0, f]
                last = state[g, QUARTER - 1, f]
                edge[g, f] = jnp.concatenate(
                    [first[SIZE:], jnp.where(low, pltpu.roll(first[:SIZE], NXC, 1), 0.0)], axis=0
                )
                prev.append(
                    jnp.concatenate(
                        [jnp.where(low, 0.0, pltpu.roll(last[SIZE:], NXC, 1)), last[:SIZE]], axis=0
                    )
                )
            for start in range(0, QUARTER, CHUNK):
                places = range(start, start + CHUNK)
                flats = [state[g, zi].reshape(FIELDS * PAIR, LANES).astype(BF16) for zi in places]
                slopes = jnp.dot(
                    jnp.concatenate(flats, axis=0), dmat[...], preferred_element_type=F32
                )
                for i, zi in enumerate(places):
                    mixed = jnp.dot(cmat[...], flats[i], preferred_element_type=F32)
                    now = [state[g, zi, f] for f in range(FIELDS)]
                    news = []
                    for f in range(FIELDS):
                        rows = slice(f * PAIR, (f + 1) * PAIR)
                        here = (i * FIELDS + f) * PAIR
                        slope = slopes[here : here + PAIR]
                        after = edge[g, f] if zi == QUARTER - 1 else state[g, zi + 1, f]
                        change = (prev[f] + after) + (
                            now[0] * slope + (jnp.tanh(mixed[rows]) + force[g, zi, f])
                        )
                        news.append(keep * now[f] + step * change)
                    for f in range(FIELDS):
                        state[g, zi, f] = news[f]
                    prev = now

    def body(turn, carry):
        running = sum(jnp.where(most[g] > turn, 1, 0) for g in range(GROUPS))
        for active in range(1, GROUPS + 1):
            pl.when(running == active)(lambda active=active: substep(turn, active))
        return carry

    lax.fori_loop(0, most[0], body, 0)


def differences(state, sums, weights, diffs):
    for zi in range(QUARTER):
        changes = []
        for g in range(GROUPS):
            end = weighted(state, g, zi, weights)
            changes.append(end - sums[g, zi])
            sums[g, zi] = end
        for sub in range(2):
            rows = jnp.concatenate([c[sub * SIZE : (sub + 1) * SIZE] for c in changes], axis=0)
            place = 2 * zi + sub
            diffs[:, place * LANES : (place + 1) * LANES] = rows.astype(BF16)


def tendency(diffs, backx):
    both = jnp.dot(diffs[...], backx[...], preferred_element_type=F32)
    return both[:, :LANES] + both[:, LANES:]


def swapped_halves(low, one, two):
    outer = jnp.where(low, one, two)
    inner = pltpu.roll(jnp.where(low, two, one), NXC, 1)
    return jnp.where(low, outer, inner), jnp.where(low, inner, outer)


def cloud_kernel(
    cloud_in, own_in, band_a_in, elem_b_in, elem_a_in, band_b_in, counts_in, level_in, back_in, coup_in, fscale_in,
    bweight_in,
    cloud_out, host_out, aux_out,
    own, band_a, elem_b, elem_a, band_b, counts, level_map, back_t, coup, fscale, bweight,
    state, force, sums, edge, dmat, cmat, counts16, backx, diffs, most, expand,
    out_buf, cloud, host_buf, aux, sems,
):
    levels = host_out.shape[1]
    sources = (
        own_in, band_a_in, elem_b_in, elem_a_in, band_b_in, counts_in, level_in, back_in, coup_in, fscale_in,
        bweight_in,
    )
    places = (own, band_a, elem_b, elem_a, band_b, counts, level_map, back_t, coup, fscale, bweight)
    copies = [
        pltpu.make_async_copy(src, dst, sems.at[FIELDS + i])
        for i, (src, dst) in enumerate(zip(sources, places))
    ]
    for copy in copies:
        copy.start()
    loads = [
        pltpu.make_async_copy(cloud_in.at[f], cloud.at[f], sems.at[f]) for f in range(FIELDS)
    ]
    for copy in loads:
        copy.start()
    r, l = row_iota(LANES, LANES), lane_iota(LANES, LANES)
    same = (r // NXC) == (l // NXC)
    ahead = same & (r % NXC == (l + 1) % NXC)
    behind = same & (r % NXC == (l + NXC - 1) % NXC)
    dmat[...] = (jnp.where(behind, 0.5, 0.0) - jnp.where(ahead, 0.5, 0.0)).astype(BF16)
    r, l = row_iota(NXC, LANES), lane_iota(NXC, LANES)
    for zi in range(QUARTER):
        for sub in range(2):
            level = sub * QUARTER + zi
            level = jnp.where(l < NXC, level, level + 2 * QUARTER)
            part = slice((2 * zi + sub) * LANES, (2 * zi + sub + 1) * LANES)
            expand[:, part] = jnp.where(r == level, 1.0, 0.0).astype(BF16)
    for copy in copies:
        copy.wait()

    counts_row = counts[...].astype(F32)
    to_slot, to_column, column = ranks(counts_row)
    to_slot = to_slot.astype(BF16)
    to_column = to_column.astype(BF16)
    over = [jnp.sum(jnp.where(counts[...] > turn, 1, 0)) for turn in range(1, SUB)]
    for g in range(GROUPS):
        most[g] = 1 + sum(jnp.where(over_turn > g * SIZE, 1, 0) for over_turn in over)
    counts_sorted = jnp.dot(
        to_slot, jnp.broadcast_to(column, (COLS, LANES)).astype(BF16), preferred_element_type=F32
    )
    for g in range(GROUPS):
        rows = counts_sorted[g * SIZE : (g + 1) * SIZE]
        counts16[g] = jnp.concatenate([rows, rows], axis=0)
    weights = [bweight[f] for f in range(FIELDS)]

    r, l = row_iota(FIELDS * PAIR, FIELDS * PAIR), lane_iota(FIELDS * PAIR, FIELDS * PAIR)
    same = (r % PAIR) == (l % PAIR)
    mixer = jnp.zeros((FIELDS * PAIR, FIELDS * PAIR), F32)
    for f in range(FIELDS):
        for other in range(FIELDS):
            here = same & (r // PAIR == f) & (l // PAIR == other)
            mixer = jnp.where(here, coup[f, other], mixer)
    cmat[...] = mixer.astype(BF16)
    padding = jnp.zeros((1, LANES - levels), F32)
    for zi in range(QUARTER):
        for sub in range(2):
            for half in range(2):
                level = (2 * half + sub) * QUARTER + zi
                row = jnp.concatenate([back_t[level : level + 1, :], padding], axis=1) * (1.0 / NXC)
                hi = row.astype(BF16)
                lo = (row - hi.astype(F32)).astype(BF16)
                first = ((2 * zi + sub) * 2 + half) * NXC
                backx[first : first + NXC, :LANES] = jnp.broadcast_to(hi, (NXC, LANES))
                backx[first : first + NXC, LANES:] = jnp.broadcast_to(lo, (NXC, LANES))

    even = lax.rem(lax.axis_index("band"), 2) == 0
    north = jnp.where(even, band_a[...], band_b[...])
    south = jnp.where(even, band_b[...], band_a[...])
    host = own[:COLS]
    kap, kap_a, kap_b, kap_n, kap_s = (
        column_of(ref[COLS : COLS + 1, :COLS]) for ref in (own, elem_a, elem_b, north, south)
    )
    face_a = 0.5 * (kap + kap_a)
    face_b = 0.5 * (kap + kap_b)
    face_n = 0.5 * (kap + jnp.concatenate([kap[1:], kap_n[:1]], axis=0))
    face_s = 0.5 * (kap + jnp.concatenate([kap_s[COLS - 1 :], kap[:-1]], axis=0))
    spread = face_a * (elem_a[:COLS] - host) + face_b * (elem_b[:COLS] - host)
    spread = spread + face_n * (jnp.concatenate([host[1:], north[0:1]], axis=0) - host)
    spread = spread + face_s * (
        jnp.concatenate([south[COLS - 1 : COLS], host[:-1]], axis=0) - host
    )

    host_sorted = permuted(to_slot, host)
    prepare_force(force, host_sorted, level_map, fscale, expand)
    spread_sorted = permuted(to_slot, spread)

    low = lane_iota(COLS, LANES) < NXC
    for copy in loads:
        copy.wait()
    for f in range(FIELDS):
        for tile in range(HALF_TILES):
            near = slice(tile * LANES, (tile + 1) * LANES)
            far = slice((tile + HALF_TILES) * LANES, (tile + HALF_TILES + 1) * LANES)
            _, sub, place = quarter_of(2 * tile)
            _, sub2, place2 = quarter_of(2 * tile + 1)
            both = jnp.concatenate(swapped_halves(low, cloud[f, :, near], cloud[f, :, far]), axis=1)
            both = jnp.dot(to_slot, both, preferred_element_type=F32)
            for g in range(GROUPS):
                rows = both[g * SIZE : (g + 1) * SIZE]
                state[g, place, f, sub * SIZE : (sub + 1) * SIZE, :] = rows[:, :LANES]
                state[g, place2, f, sub2 * SIZE : (sub2 + 1) * SIZE, :] = rows[:, LANES:]
    for g in range(GROUPS):
        for zi in range(QUARTER):
            sums[g, zi] = weighted(state, g, zi, weights)

    advance_window(state, force, counts16, most, edge, dmat, cmat)
    differences(state, sums, weights, diffs)
    tend_sorted = tendency(diffs, backx)
    host_sorted = host_sorted + (tend_sorted[:, :levels] + spread_sorted)
    prepare_force(force, host_sorted, level_map, fscale, expand)
    tend = permuted(to_column, tend_sorted)
    host = host + (tend[:, :levels] + spread)
    host_buf[...] = host
    sending = [pltpu.make_async_copy(host_buf, host_out, sems.at[0])]
    sending[0].start()
    advance_window(state, force, counts16, most, edge, dmat, cmat)
    differences(state, sums, weights, diffs)
    for fields in (range(0, FIELDS // 2), range(FIELDS // 2, FIELDS)):
        if fields[0] > 0:
            tend = permuted(to_column, tendency(diffs, backx))
            zero = jnp.zeros((1, levels), F32)
            base = host + (tend[:, :levels] - (face_a + face_b + face_n + face_s) * host)
            base = base + face_n * jnp.concatenate([host[1:], zero], axis=0)
            base = base + face_s * jnp.concatenate([zero, host[:-1]], axis=0)
            room = jnp.zeros((COLS, LANES - levels - 4), F32)
            aux[...] = jnp.concatenate([base, face_a, face_b, face_n, face_s, room], axis=1)
        for tile in range(HALF_TILES):
            near = slice(tile * LANES, (tile + 1) * LANES)
            far = slice((tile + HALF_TILES) * LANES, (tile + HALF_TILES + 1) * LANES)
            _, sub, place = quarter_of(2 * tile)
            _, sub2, place2 = quarter_of(2 * tile + 1)
            for f in fields:
                rows = jnp.concatenate(
                    [
                        jnp.concatenate(
                            [
                                state[g, place, f, sub * SIZE : (sub + 1) * SIZE, :],
                                state[g, place2, f, sub2 * SIZE : (sub2 + 1) * SIZE, :],
                            ],
                            axis=1,
                        )
                        for g in range(GROUPS)
                    ],
                    axis=0,
                )
                out = jnp.dot(to_column, rows.astype(BF16), preferred_element_type=F32).astype(BF16)
                one, two = swapped_halves(low, out[:, :LANES], out[:, LANES:])
                out_buf[f, :, near] = one
                out_buf[f, :, far] = two
        for f in fields:
            copy = pltpu.make_async_copy(out_buf.at[f], cloud_out.at[f], sems.at[len(sending)])
            copy.start()
            sending.append(copy)
    copy = pltpu.make_async_copy(aux, aux_out, sems.at[len(sending)])
    copy.start()
    sending.append(copy)
    for copy in sending:
        copy.wait()


def host_kernel(aux, band_a, elem_a, band_b, elem_b, out):
    levels = out.shape[1]
    face_a, face_b, face_n, face_s = (aux[:, levels + i : levels + i + 1] for i in range(4))
    total = aux[:, :levels] + (face_a * elem_a[...] + face_b * elem_b[...])
    even = lax.rem(lax.axis_index("band"), 2) == 0
    north = jnp.where(even, band_a[0:1], band_b[0:1])
    south = jnp.where(even, band_b[COLS - 1 : COLS], band_a[COLS - 1 : COLS])
    rows = row_iota(*total.shape)
    total = total + jnp.where(rows == COLS - 1, face_n * north, 0.0)
    out[...] = total + jnp.where(rows == 0, face_s * south, 0.0)


def neighbours(block):
    found = []
    for odd in range(2):
        for axis in ("band", "elem"):
            count = lax.axis_size(axis)
            pairs = [(i, (i + 1 - 2 * ((i + odd) % 2)) % count) for i in range(count)]
            found.append(lax.ppermute(block, axis, pairs))
    return found


VMEM = pl.BlockSpec(memory_space=pltpu.VMEM)
SMEM = pl.BlockSpec(memory_space=pltpu.SMEM)
HBM = pl.BlockSpec(memory_space=pl.ANY)
STATE = (GROUPS, QUARTER, FIELDS, PAIR, LANES)


def body(
    crm_state, host_state, kappa, substeps, coupling, level_map, field_scale, back_map, back_weight
):
    levels = host_state.shape[0]
    cloud = jnp.transpose(crm_state[0], (1, 0, 2))
    host = jnp.transpose(host_state[:, 0, :], (1, 0))
    own = jnp.concatenate([host, jnp.pad(kappa, ((0, 0), (0, levels - COLS)))], axis=0)
    band_a, elem_a, band_b, elem_b = neighbours(own)
    near = (band_a, elem_b, elem_a, band_b)
    cloud_out, host, aux = pl.pallas_call(
        cloud_kernel,
        out_shape=(
            jax.ShapeDtypeStruct(cloud.shape, BF16),
            jax.ShapeDtypeStruct((COLS, levels), F32),
            jax.ShapeDtypeStruct((COLS, LANES), F32),
        ),
        in_specs=[HBM] * 12,
        out_specs=(HBM,) * 3,
        scratch_shapes=[pltpu.VMEM(own.shape, F32)] * 5
        + [
            pltpu.VMEM((1, COLS), jnp.int32),
            pltpu.VMEM((NZC, levels), F32),
            pltpu.VMEM((NZC, levels), F32),
            pltpu.SMEM((FIELDS, FIELDS), F32),
            pltpu.SMEM((FIELDS,), F32),
            pltpu.SMEM((FIELDS,), F32),
            pltpu.VMEM(STATE, F32),
            pltpu.VMEM(STATE, F32),
            pltpu.VMEM((GROUPS, QUARTER, PAIR, LANES), F32),
            pltpu.VMEM((GROUPS, FIELDS, PAIR, LANES), F32),
            pltpu.VMEM((LANES, LANES), BF16),
            pltpu.VMEM((FIELDS * PAIR, FIELDS * PAIR), BF16),
            pltpu.VMEM((GROUPS, PAIR, LANES), F32),
            pltpu.VMEM((CELLS, 2 * LANES), BF16),
            pltpu.VMEM((COLS, CELLS), BF16),
            pltpu.SMEM((GROUPS,), jnp.int32),
            pltpu.VMEM((NXC, CELLS), BF16),
            pltpu.VMEM((FIELDS, COLS, CELLS), BF16),
            pltpu.VMEM((FIELDS, COLS, CELLS), BF16),
            pltpu.VMEM((COLS, levels), F32),
            pltpu.VMEM((COLS, LANES), F32),
            pltpu.SemaphoreType.DMA((FIELDS + 11,)),
        ],
        compiler_params=pltpu.CompilerParams(vmem_limit_bytes=56 * 1024 * 1024),
        name="cloud_windows",
    )(cloud, own, *near, substeps, level_map, back_map.T, coupling, field_scale, back_weight)
    host = pl.pallas_call(
        host_kernel,
        out_shape=jax.ShapeDtypeStruct((COLS, levels), F32),
        in_specs=[VMEM] * 5,
        out_specs=VMEM,
        compiler_params=pltpu.CompilerParams(vmem_limit_bytes=1024 * 1024),
        name="host_section",
    )(aux, *neighbours(host))
    crm_final = jnp.transpose(cloud_out, (1, 0, 2))[None]
    host_final = jnp.transpose(host, (1, 0))[:, None, :]
    return (crm_final, host_final)


def solution(mesh):
    return jax.shard_map(
        body,
        mesh=mesh,
        in_specs=(
            P("elem", "band", None, None),
            P(None, "elem", "band"),
            P("elem", "band"),
            P("elem", "band"),
            P(),
            P(),
            P(),
            P(),
            P(),
        ),
        out_specs=(P("elem", "band", None, None), P(None, "elem", "band")),
        check_vma=False,
    )
```
